32 devices in a mesh: dp: 2 (over y), expert: 16 (over z, x, core).
Axes of the slice: x: 2, y: 2, z: 4, core: 2. Of those that a mesh axis runs over, the one named last changes fastest.
Arguments:
- tokens: bfloat16 [4096, 2560], P(('dp', 'expert')), may hold values from -6 to 6
- expert_ids: int32 [4096, 6], P(('dp', 'expert')), may hold values from 0 to 159, as said below
- gate_values: bfloat16 [4096, 6], P(('dp', 'expert')), may hold values from 0.29882812 to 1.59375
- gate_weight: bfloat16 [16, 768, 2560], P('expert', 'dp'), may hold values from -0.125 to 0.125
- up_weight: bfloat16 [16, 768, 2560], P('expert', 'dp'), may hold values from -0.125 to 0.125
- down_weight: bfloat16 [16, 768, 2560], P('expert', 'dp'), may hold values from -0.21875 to 0.21875
- first_moment: bfloat16 [16, 768, 2560], P('expert', 'dp'), may hold values from -6 to 6
- second_moment: bfloat16 [16, 768, 2560], P('expert', 'dp'), may hold values from 0.5 to 8
Outputs:
- new_down: bfloat16 [16, 768, 2560], P('expert', 'dp')
- new_first: bfloat16 [16, 768, 2560], P('expert', 'dp')
- new_second: bfloat16 [16, 768, 2560], P('expert', 'dp')
The draws below stay inside these ranges and needn't reach their ends.
Inputs may be any that keep to these rules, and one draw needn't show every extreme that they name: `expert_ids`: each row names 6 different experts; among the rows of one device no expert is named more than 6 times. One expert below 16 is named exactly 6 times by the rows of every device, and in each device's rows another one too. In the rows of each device exactly 12 rows name only experts below 16, and the other rows name none of them. Ids of 16 or more name experts outside this computation.
All inputs are finite; a program needn't handle non-finite values.
Results may differ from the reference program's by a relative error of at most 0.015.
Values may be sent and summed in bfloat16 or wider, within the bound.
No kernel may reach another device: no remote copies, remote signals or barrier semaphores. Data moves between devices by JAX's collectives and lax.ppermute only.
A program may use at most 128 MiB of HBM per device.

```python
import math
from functools import partial
import jax
import jax.numpy as jnp
from jax import lax

D = 2560
H = 768
EXP_ALL = 160
TOP = 6
TOK_DEV = 128
CAP = 6
EXPERTS = 16
HOT_ROWS = 12
TOKENS = 4096
N_DP = 2
N_EXPERT = 16


def fill_block(block_key, expert_count, row_count, forced):
    pool_size = expert_count * CAP
    entry_ids = jnp.arange(pool_size, dtype=jnp.int32)
    owners = entry_ids // CAP
    scores = jax.random.randint(block_key, (pool_size,), 0, 2 ** 16, dtype=jnp.int32) * pool_size + entry_ids
    scores = jnp.where(forced[owners], entry_ids - pool_size, scores)
    ranking = jnp.argsort(scores, stable=True)
    picked = jnp.sort(owners[ranking[:row_count * TOP]])
    return jnp.transpose(picked.reshape(TOP, row_count))


def draw_expert_ids(key, part):
    key = jax.random.fold_in(key, 11)
    blocks = TOKENS // TOK_DEV
    favored = jax.random.randint(jax.random.fold_in(key, 1), (), 0, EXPERTS, dtype=jnp.int32)
    block_keys = jax.random.split(jax.random.fold_in(key, 2), blocks)
    expert_range = jnp.arange(EXPERTS, dtype=jnp.int32)

    def one_block(block_key):
        sub_keys = jax.random.split(block_key, 4)
        second = (favored + 1 + jax.random.randint(sub_keys[0], (), 0, EXPERTS - 1, dtype=jnp.int32)) % EXPERTS
        marked = (expert_range == favored) | (expert_range == second)
        upper_rect = fill_block(sub_keys[1], EXPERTS, HOT_ROWS, marked)
        no_force = jnp.zeros((EXP_ALL - EXPERTS,), dtype=jnp.bool_)
        lower_rect = fill_block(sub_keys[2], EXP_ALL - EXPERTS, TOK_DEV - HOT_ROWS, no_force) + EXPERTS
        joined = jnp.concatenate([upper_rect, lower_rect], axis=0)
        shuffled = jax.random.permutation(sub_keys[3], joined, axis=0)
        column_key = jax.random.fold_in(sub_keys[3], 5)
        column_scores = jax.random.randint(column_key, (TOK_DEV, TOP), 0, 2 ** 16, dtype=jnp.int32) * TOP
        column_scores = column_scores + jnp.arange(TOP, dtype=jnp.int32)[None, :]
        column_order = jnp.argsort(column_scores, axis=1, stable=True)
        return jnp.take_along_axis(shuffled, column_order, axis=1)
    return jax.vmap(one_block)(block_keys).reshape(TOKENS, TOP).astype(jnp.int32)


def steps_of(own_key, extent, cuts, least, largest):
    factor_of, own = 1.0, jax.random.fold_in(own_key, 6)
    for dim, blocks in cuts:
        heights = jnp.exp(jax.random.uniform(jax.random.fold_in(own, dim), (blocks,), jnp.float32, least / len(cuts), largest / len(cuts)))
        factor_of = factor_of * jnp.repeat(heights, extent[dim] // blocks).reshape([-1 if axis == dim else 1 for axis in range(len(extent))])
    return factor_of


def noise(key, shape, scale, reach, cuts=(), kind=jnp.bfloat16):
    values = scale * jax.random.normal(key, shape, jnp.float32)
    if cuts:
        values = values * steps_of(key, shape, cuts, -0.22, 0.18)
    return jnp.clip(values, -reach, reach).astype(kind)


def setup_inputs(seed: int = 0) -> dict:
    streams_of = jax.random.split(jax.random.key(seed), 9)
    return {
        "tokens": noise(streams_of[0], (TOKENS, D), 1.0, 6.0, ((0, 32),)),
        "expert_ids": draw_expert_ids(jax.random.fold_in(streams_of[8], 71), 0),
        "gate_values": jnp.clip(0.29882812 + 1.2949219 * jax.random.uniform(streams_of[2], (TOKENS, TOP), jnp.float32) ** steps_of(streams_of[2], (TOKENS, TOP), ((0, 32),), -0.2, 0.2), 0.29882812, 1.59375).astype(jnp.bfloat16),
        "gate_weight": noise(streams_of[3], (EXPERTS, H, D), D ** -0.5, 0.125, ((0, 16), (1, 2))),
        "up_weight": noise(streams_of[4], (EXPERTS, H, D), D ** -0.5, 0.125, ((0, 16), (1, 2))),
        "down_weight": noise(streams_of[5], (EXPERTS, H, D), H ** -0.5, 0.21875, ((0, 16), (1, 2))),
        "first_moment": noise(streams_of[6], (EXPERTS, H, D), 1.0, 6.0, ((0, 16), (1, 2))),
        "second_moment": jnp.clip(jnp.exp(math.log(8.0) - 2.7725887 * jax.random.uniform(streams_of[7], (EXPERTS, H, D), jnp.float32) ** steps_of(streams_of[7], (EXPERTS, H, D), ((0, 16), (1, 2)), -0.2, 0.2)), 0.5, 8.0).astype(jnp.bfloat16),
    }


first_decay = 0.9
second_decay = 0.95
learn_rate = 0.00024
weight_decay = 0.1
adam_epsilon = 1e-08
adam_count = 100.0

def slot_table(id_block, gate_block, experts, capacity):
    numbers = jnp.arange(experts, dtype=jnp.int32)
    matches = id_block[:, :, None] == numbers[None, None, :]
    member = lax.optimization_barrier(jnp.sum(matches.astype(jnp.int32), axis=1))
    chosen = lax.optimization_barrier(jnp.sum(jnp.where(matches, gate_block[:, :, None].astype(jnp.float32), jnp.float32(0.0)), axis=1))
    position = jnp.cumsum(member, axis=0) - member
    slot_ids = jnp.arange(capacity, dtype=jnp.int32)
    onehot = member[:, :, None] * (position[:, :, None] == slot_ids[None, None, :]).astype(jnp.int32)
    return (onehot, chosen)

def expert_hidden(expert_rows, gate_rows, up_rows):
    gate_part = jnp.dot(expert_rows, gate_rows.T, preferred_element_type=jnp.float32)
    up_part = jnp.dot(expert_rows, up_rows.T, preferred_element_type=jnp.float32)
    return (jax.nn.silu(gate_part) * up_part).astype(jnp.bfloat16)

def adam_update(gradient, weight_rows, first_rows, second_rows):
    first_new = first_decay * first_rows.astype(jnp.float32) + (1.0 - first_decay) * gradient
    second_new = second_decay * second_rows.astype(jnp.float32) + (1.0 - second_decay) * gradient * gradient
    first_hat = first_new / (1.0 - first_decay ** adam_count)
    second_hat = second_new / (1.0 - second_decay ** adam_count)
    weight_new = weight_rows.astype(jnp.float32) * (1.0 - learn_rate * weight_decay) - learn_rate * first_hat / (jnp.sqrt(second_hat) + adam_epsilon)
    return (weight_new.astype(jnp.bfloat16), first_new.astype(jnp.bfloat16), second_new.astype(jnp.bfloat16))

def reference(tokens, expert_ids, gate_values, gate_weight, up_weight, down_weight, first_moment, second_moment):
    blocks = N_DP * N_EXPERT
    experts = N_EXPERT
    id_blocks = expert_ids.reshape(blocks, TOK_DEV, TOP)
    gate_blocks = gate_values.reshape(blocks, TOK_DEV, TOP)
    onehot, chosen = jax.vmap(partial(slot_table, experts=experts, capacity=CAP))(id_blocks, gate_blocks)
    local_index = jnp.arange(TOK_DEV, dtype=jnp.int32)
    token_index = lax.optimization_barrier(jnp.sum(onehot * local_index[None, :, None, None], axis=1))
    block_start = jnp.arange(blocks, dtype=jnp.int32) * TOK_DEV
    global_index = (token_index + block_start[:, None, None]).astype(jnp.int32)
    occupied_all = lax.optimization_barrier(jnp.sum(onehot, axis=1))
    slot_gate = lax.optimization_barrier(jnp.sum(onehot.astype(jnp.float32) * chosen[:, :, :, None], axis=1))
    by_expert = (jnp.transpose(global_index, (1, 0, 2)), jnp.transpose(occupied_all, (1, 0, 2)), jnp.transpose(slot_gate, (1, 0, 2)), gate_weight, up_weight)

    def forward_step(mixed, inputs):
        picked, occupied, scales, gate_rows, up_rows, down_rows = inputs
        flat_index = picked.reshape(-1).astype(jnp.int32)
        expert_rows = tokens[flat_index] * occupied.reshape(-1, 1).astype(jnp.bfloat16)
        hidden = expert_hidden(expert_rows, gate_rows, up_rows)
        outputs = jnp.dot(hidden, down_rows, preferred_element_type=jnp.float32).astype(jnp.bfloat16)
        mixed = mixed.at[flat_index].add(scales.reshape(-1, 1) * outputs.astype(jnp.float32))
        return (mixed, None)
    mixed, unused = lax.scan(forward_step, jnp.zeros(tokens.shape, jnp.float32), by_expert + (down_weight,))
    cotangent = jnp.tanh(tokens.astype(jnp.float32) + mixed).astype(jnp.bfloat16)

    def update_step(running, inputs):
        picked, occupied, scales, gate_rows, up_rows, down_rows, first_rows, second_rows = inputs
        flat_index = picked.reshape(-1).astype(jnp.int32)
        expert_rows = tokens[flat_index] * occupied.reshape(-1, 1).astype(jnp.bfloat16)
        hidden = expert_hidden(expert_rows, gate_rows, up_rows)
        weighted = (scales.reshape(-1, 1) * cotangent[flat_index].astype(jnp.float32)).astype(jnp.bfloat16)
        hidden_rows = hidden.reshape(N_DP, N_EXPERT * CAP, -1).astype(jnp.float32)
        weighted_dp = weighted.reshape(N_DP, N_EXPERT * CAP, -1).astype(jnp.float32)
        terms = jnp.einsum('drh,drc->dhc', hidden_rows, weighted_dp).astype(jnp.bfloat16)
        gradient = lax.optimization_barrier(jnp.sum(terms.astype(jnp.float32), axis=0))
        return (running, adam_update(gradient, down_rows, first_rows, second_rows))
    unused_carry, results = lax.scan(update_step, jnp.float32(0.0), by_expert + (down_weight, first_moment, second_moment))
    return (results[0], results[1], results[2])
```

```python
import jax
import jax.numpy as jnp
from jax import lax
from jax.sharding import PartitionSpec as P

CAP = 6


first_decay = 0.9
second_decay = 0.95
learn_rate = 0.00024
weight_decay = 0.1
adam_epsilon = 1e-08
adam_count = 100.0


def slot_table(id_block, gate_block, experts, capacity):
    numbers = jnp.arange(experts, dtype=jnp.int32)
    matches = id_block[:, :, None] == numbers[None, None, :]
    member = jnp.sum(matches.astype(jnp.int32), axis=1)
    chosen = jnp.sum(
        jnp.where(matches, gate_block[:, :, None].astype(jnp.float32), jnp.float32(0.0)), axis=1
    )
    position = jnp.cumsum(member, axis=0) - member
    slot_ids = jnp.arange(capacity, dtype=jnp.int32)
    onehot = member[:, :, None] * (position[:, :, None] == slot_ids[None, None, :]).astype(
        jnp.int32
    )
    return (onehot, chosen)


def expert_hidden(expert_rows, gate_rows, up_rows):
    contract = (((1,), (1,)), ((), ()))
    gate_part = lax.dot_general(
        expert_rows, gate_rows, contract, preferred_element_type=jnp.float32
    )
    up_part = lax.dot_general(expert_rows, up_rows, contract, preferred_element_type=jnp.float32)
    return (jax.nn.silu(gate_part) * up_part).astype(jnp.bfloat16)


def adam_update(gradient, weight_rows, first_rows, second_rows):
    first_new = first_decay * first_rows.astype(jnp.float32) + (1.0 - first_decay) * gradient
    second_new = (
        second_decay * second_rows.astype(jnp.float32) + (1.0 - second_decay) * gradient * gradient
    )
    first_hat = first_new / (1.0 - first_decay**adam_count)
    second_hat = second_new / (1.0 - second_decay**adam_count)
    weight_new = weight_rows.astype(jnp.float32) * (
        1.0 - learn_rate * weight_decay
    ) - learn_rate * first_hat / (jnp.sqrt(second_hat) + adam_epsilon)
    return (
        weight_new.astype(jnp.bfloat16),
        first_new.astype(jnp.bfloat16),
        second_new.astype(jnp.bfloat16),
    )


def slot_plan(
    tokens,
    expert_ids,
    gate_values,
    gate_weight,
    up_weight,
    down_weight,
    first_moment,
    second_moment,
):
    experts = lax.axis_size("expert")
    tok_count, model_width = tokens.shape
    capacity = CAP
    slot_count = experts * capacity
    onehot, chosen = slot_table(expert_ids, gate_values, experts, capacity)
    dispatch_map = onehot.reshape(tok_count, slot_count).astype(jnp.bfloat16)
    combine_map = (
        (onehot.astype(jnp.float32) * chosen[:, :, None])
        .reshape(tok_count, slot_count)
        .astype(jnp.bfloat16)
    )
    over_tokens = (((0,), (0,)), ((), ()))
    outgoing = lax.dot_general(
        dispatch_map, tokens, over_tokens, preferred_element_type=jnp.float32
    ).astype(jnp.bfloat16)
    arrived = lax.all_to_all(
        outgoing.reshape(experts, capacity, model_width),
        "expert",
        split_axis=0,
        concat_axis=0,
        tiled=True,
    )
    arrived = arrived.reshape(slot_count, model_width)
    gate_full, up_full, down_full = (
        lax.all_gather(gate_weight, "dp", axis=1, tiled=True),
        lax.all_gather(up_weight, "dp", axis=1, tiled=True),
        lax.all_gather(down_weight, "dp", axis=1, tiled=True),
    )
    hidden = expert_hidden(arrived, gate_full[0], up_full[0])
    outputs = jnp.dot(hidden, down_full[0], preferred_element_type=jnp.float32).astype(jnp.bfloat16)
    returned = lax.all_to_all(
        outputs.reshape(experts, capacity, model_width),
        "expert",
        split_axis=0,
        concat_axis=0,
        tiled=True,
    )
    returned = returned.reshape(slot_count, model_width)
    mixed = jnp.dot(combine_map, returned, preferred_element_type=jnp.float32)
    cotangent = jnp.tanh(tokens.astype(jnp.float32) + mixed).astype(jnp.bfloat16)
    weighted = lax.dot_general(
        combine_map, cotangent, over_tokens, preferred_element_type=jnp.float32
    ).astype(jnp.bfloat16)
    arrived_grad = lax.all_to_all(
        weighted.reshape(experts, capacity, model_width),
        "expert",
        split_axis=0,
        concat_axis=0,
        tiled=True,
    )
    arrived_grad = arrived_grad.reshape(slot_count, model_width)
    gradient = lax.psum_scatter(
        lax.dot_general(
            hidden, arrived_grad, over_tokens, preferred_element_type=jnp.float32
        ).astype(jnp.bfloat16),
        "dp",
        scatter_dimension=0,
        tiled=True,
    ).astype(jnp.float32)
    new_down, new_first, new_second = adam_update(
        gradient, down_weight[0], first_moment[0], second_moment[0]
    )
    return (new_down[None], new_first[None], new_second[None])


AXES = ("dp", "expert")
CORE = (1,)
PLANE = (2, 16, 18)
LINE = (4, 8, 12)


def swap(block, mask):
    count = lax.axis_size(AXES)
    return lax.ppermute(block, AXES, [(i, i ^ mask) for i in range(count)])


def spread(block):
    for masks in (LINE, PLANE, CORE):
        block = jnp.concatenate([block] + [swap(block, mask) for mask in masks], axis=0)
    return block


def collect(terms):
    total = terms
    for masks in (CORE, PLANE, LINE):
        parts = jnp.split(total.astype(jnp.bfloat16), len(masks) + 1, axis=0)
        own = jnp.split(total, len(masks) + 1, axis=0)[0].astype(jnp.float32)
        for part, mask in zip(parts[1:], masks):
            own = own + swap(part, mask).astype(jnp.float32)
        total = own
    return total


def dense_plan(
    tokens,
    expert_ids,
    gate_values,
    gate_weight,
    up_weight,
    down_weight,
    first_moment,
    second_moment,
):
    experts = lax.axis_size("expert")
    width = tokens.shape[1]
    hot_rows = experts * 3 // 4
    numbers = jnp.arange(experts, dtype=jnp.int32)
    matches = expert_ids[:, :, None] == numbers
    gates = jnp.sum(jnp.where(matches, gate_values[:, :, None], 0), axis=1)
    hot = jnp.any(expert_ids < experts, axis=1).astype(jnp.int32)
    rank = jnp.cumsum(hot) - hot
    place = jnp.arange(hot_rows, dtype=jnp.int32)
    pick = ((rank[None, :] == place[:, None]) & (hot[None, :] == 1)).astype(jnp.bfloat16)
    hot_tokens = jnp.dot(pick, tokens, preferred_element_type=jnp.float32).astype(jnp.bfloat16)
    hot_gates = jnp.dot(pick, gates, preferred_element_type=jnp.float32).astype(jnp.bfloat16)
    hot_gates = jnp.pad(hot_gates, ((0, 0), (0, 128 - experts)))
    packed = spread(jnp.concatenate([hot_tokens, hot_gates], axis=1))
    rows = packed[:, :width]
    mine = numbers == lax.axis_index("expert")
    gate = jnp.sum(
        jnp.where(mine, packed[:, width : width + experts].astype(jnp.float32), 0.0),
        axis=1,
        keepdims=True,
    )
    contract = (((1,), (1,)), ((), ()))
    gate_part = lax.dot_general(rows, gate_weight[0], contract, preferred_element_type=jnp.float32)
    up_part = lax.dot_general(rows, up_weight[0], contract, preferred_element_type=jnp.float32)
    hidden = (gate * (jax.nn.silu(gate_part) * up_part)).astype(jnp.bfloat16)
    terms = jnp.dot(hidden, down_weight[0], preferred_element_type=jnp.float32)
    mixed = collect(terms)
    cotangent = jnp.tanh(hot_tokens.astype(jnp.float32) + mixed).astype(jnp.bfloat16)
    gradient = lax.dot_general(
        hidden, spread(cotangent), (((0,), (0,)), ((), ())), preferred_element_type=jnp.float32
    )
    new_down, new_first, new_second = adam_update(
        gradient, down_weight[0], first_moment[0], second_moment[0]
    )
    return (new_down[None], new_first[None], new_second[None])


def solution(mesh):
    in_specs = (
        P(("dp", "expert"), None),
        P(("dp", "expert"), None),
        P(("dp", "expert"), None),
        P("expert", "dp", None),
        P("expert", "dp", None),
        P("expert", "dp", None),
        P("expert", "dp", None),
        P("expert", "dp", None),
    )
    out_specs = (P("expert", "dp", None), P("expert", "dp", None), P("expert", "dp", None))
    small = mesh.shape["dp"] == 2 and mesh.shape["expert"] == 16
    local = dense_plan if small else slot_plan
    return jax.shard_map(local, mesh=mesh, in_specs=in_specs, out_specs=out_specs, check_vma=False)
```

```python
import functools

import jax
import jax.numpy as jnp
from jax import lax
from jax.experimental import pallas as pl
from jax.experimental.pallas import tpu as pltpu
from jax.sharding import PartitionSpec as P

CAP = 6


first_decay = 0.9
second_decay = 0.95
learn_rate = 0.00024
weight_decay = 0.1
adam_epsilon = 1e-08
adam_count = 100.0


def slot_table(id_block, gate_block, experts, capacity):
    numbers = jnp.arange(experts, dtype=jnp.int32)
    matches = id_block[:, :, None] == numbers[None, None, :]
    member = jnp.sum(matches.astype(jnp.int32), axis=1)
    chosen = jnp.sum(
        jnp.where(matches, gate_block[:, :, None].astype(jnp.float32), jnp.float32(0.0)), axis=1
    )
    position = jnp.cumsum(member, axis=0) - member
    slot_ids = jnp.arange(capacity, dtype=jnp.int32)
    onehot = member[:, :, None] * (position[:, :, None] == slot_ids[None, None, :]).astype(
        jnp.int32
    )
    return (onehot, chosen)


def expert_hidden(expert_rows, gate_rows, up_rows):
    contract = (((1,), (1,)), ((), ()))
    gate_part = lax.dot_general(
        expert_rows, gate_rows, contract, preferred_element_type=jnp.float32
    )
    up_part = lax.dot_general(expert_rows, up_rows, contract, preferred_element_type=jnp.float32)
    return (jax.nn.silu(gate_part) * up_part).astype(jnp.bfloat16)


def adam_update(gradient, weight_rows, first_rows, second_rows):
    first_new = first_decay * first_rows.astype(jnp.float32) + (1.0 - first_decay) * gradient
    second_new = (
        second_decay * second_rows.astype(jnp.float32) + (1.0 - second_decay) * gradient * gradient
    )
    first_hat = first_new / (1.0 - first_decay**adam_count)
    second_hat = second_new / (1.0 - second_decay**adam_count)
    weight_new = weight_rows.astype(jnp.float32) * (
        1.0 - learn_rate * weight_decay
    ) - learn_rate * first_hat / (jnp.sqrt(second_hat) + adam_epsilon)
    return (
        weight_new.astype(jnp.bfloat16),
        first_new.astype(jnp.bfloat16),
        second_new.astype(jnp.bfloat16),
    )


def slot_plan(
    tokens,
    expert_ids,
    gate_values,
    gate_weight,
    up_weight,
    down_weight,
    first_moment,
    second_moment,
):
    experts = lax.axis_size("expert")
    tok_count, model_width = tokens.shape
    capacity = CAP
    slot_count = experts * capacity
    onehot, chosen = slot_table(expert_ids, gate_values, experts, capacity)
    dispatch_map = onehot.reshape(tok_count, slot_count).astype(jnp.bfloat16)
    combine_map = (
        (onehot.astype(jnp.float32) * chosen[:, :, None])
        .reshape(tok_count, slot_count)
        .astype(jnp.bfloat16)
    )
    over_tokens = (((0,), (0,)), ((), ()))
    outgoing = lax.dot_general(
        dispatch_map, tokens, over_tokens, preferred_element_type=jnp.float32
    ).astype(jnp.bfloat16)
    arrived = lax.all_to_all(
        outgoing.reshape(experts, capacity, model_width),
        "expert",
        split_axis=0,
        concat_axis=0,
        tiled=True,
    )
    arrived = arrived.reshape(slot_count, model_width)
    gate_full, up_full, down_full = (
        lax.all_gather(gate_weight, "dp", axis=1, tiled=True),
        lax.all_gather(up_weight, "dp", axis=1, tiled=True),
        lax.all_gather(down_weight, "dp", axis=1, tiled=True),
    )
    hidden = expert_hidden(arrived, gate_full[0], up_full[0])
    outputs = jnp.dot(hidden, down_full[0], preferred_element_type=jnp.float32).astype(jnp.bfloat16)
    returned = lax.all_to_all(
        outputs.reshape(experts, capacity, model_width),
        "expert",
        split_axis=0,
        concat_axis=0,
        tiled=True,
    )
    returned = returned.reshape(slot_count, model_width)
    mixed = jnp.dot(combine_map, returned, preferred_element_type=jnp.float32)
    cotangent = jnp.tanh(tokens.astype(jnp.float32) + mixed).astype(jnp.bfloat16)
    weighted = lax.dot_general(
        combine_map, cotangent, over_tokens, preferred_element_type=jnp.float32
    ).astype(jnp.bfloat16)
    arrived_grad = lax.all_to_all(
        weighted.reshape(experts, capacity, model_width),
        "expert",
        split_axis=0,
        concat_axis=0,
        tiled=True,
    )
    arrived_grad = arrived_grad.reshape(slot_count, model_width)
    gradient = lax.psum_scatter(
        lax.dot_general(
            hidden, arrived_grad, over_tokens, preferred_element_type=jnp.float32
        ).astype(jnp.bfloat16),
        "dp",
        scatter_dimension=0,
        tiled=True,
    ).astype(jnp.float32)
    new_down, new_first, new_second = adam_update(
        gradient, down_weight[0], first_moment[0], second_moment[0]
    )
    return (new_down[None], new_first[None], new_second[None])


AXES = ("dp", "expert")
CORE = 1
PLANE = (2, 16, 18)
LINE = (4, 8, 12)
CHUNKS = 1
LANES = 128
MIB = 1024 * 1024


def swap(block, mask):
    count = lax.axis_size(AXES)
    return lax.ppermute(block, AXES, [(i, i ^ mask) for i in range(count)])


def spread(block):
    block = jnp.concatenate([block] + [swap(block, mask) for mask in LINE], axis=0)
    pieces = [block] + [swap(block, mask) for mask in PLANE]
    return pieces + [swap(piece, CORE) for piece in pieces]


def add_parts(own, other_parts):
    total = own.astype(jnp.float32)
    for part in other_parts:
        total = total + part.astype(jnp.float32)
    return total


def collect(own, other):
    total = add_parts(own, [swap(other, CORE)])
    for masks in (PLANE, LINE):
        parts = jnp.split(total, len(masks) + 1, axis=0)
        sent = [swap(part.astype(jnp.bfloat16), mask) for part, mask in zip(parts[1:], masks)]
        total = add_parts(parts[0], sent)
    return total


def expert_kernel(chunks, *refs):
    pieces = refs[: 8 * chunks]
    gate_ref, up_ref, down_ref, sel_ref = refs[8 * chunks : 8 * chunks + 4]
    outs = refs[8 * chunks + 4 : 8 * chunks + 4 + 2 * chunks]
    hidden_t_ref, rows, gates, gate_vm, up_vm, down_vm, sems = refs[8 * chunks + 4 + 2 * chunks :]
    count, width = rows.shape
    part = count // 8
    span = width // chunks
    copies = []
    for c in range(chunks):
        for p in range(8):
            src = pieces[8 * c + p]
            sem = sems.at[8 * c + p]
            if c == 0:
                copies.append(
                    pltpu.make_async_copy(
                        src.at[:, pl.ds(span, LANES)],
                        gates.at[pl.ds(p * part, part)],
                        sems.at[8 * chunks + p],
                    )
                )
                src = src.at[:, pl.ds(0, span)]
            copies.append(
                pltpu.make_async_copy(
                    src, rows.at[pl.ds(p * part, part), pl.ds(c * span, span)], sem
                )
            )
    gate_copy = pltpu.make_async_copy(gate_ref, gate_vm, sems.at[8 * chunks + 8])
    up_copy = pltpu.make_async_copy(up_ref, up_vm, sems.at[8 * chunks + 9])
    down_copy = pltpu.make_async_copy(down_ref, down_vm, sems.at[8 * chunks + 10])
    for copy in copies + [gate_copy, up_copy, down_copy]:
        copy.start()
    for copy in copies + [gate_copy]:
        copy.wait()
    contract = (((1,), (1,)), ((), ()))
    gate = jnp.sum(gates[...].astype(jnp.float32) * sel_ref[...], axis=1, keepdims=True)
    gate_part = lax.dot_general(
        rows[...], gate_vm[...], contract, preferred_element_type=jnp.float32
    )
    up_copy.wait()
    up_part = lax.dot_general(rows[...], up_vm[...], contract, preferred_element_type=jnp.float32)
    hidden = gate * (jax.nn.silu(gate_part) * up_part)
    hidden_t_ref[...] = hidden.T.astype(jnp.bfloat16)
    hidden = hidden.astype(jnp.bfloat16)
    down_copy.wait()
    for c in range(chunks):
        terms = jnp.dot(
            hidden, down_vm[:, c * span : (c + 1) * span], preferred_element_type=jnp.float32
        ).astype(jnp.bfloat16)
        outs[2 * c][...] = terms[: count // 2]
        outs[2 * c + 1][...] = terms[count // 2 :]


def expert_terms(pieces, gate_weight, up_weight, down_weight, sel):
    chunks = len(pieces)
    part = pieces[0][0].shape[0]
    units, width = gate_weight.shape
    count = 8 * part
    span = width // chunks
    flat = [piece for chunk in pieces for piece in chunk]
    half = jax.ShapeDtypeStruct((count // 2, span), jnp.bfloat16)
    anywhere = pl.BlockSpec(memory_space=pl.ANY)
    in_vmem = pl.BlockSpec(memory_space=pltpu.VMEM)
    outs = pl.pallas_call(
        functools.partial(expert_kernel, chunks),
        out_shape=[half] * (2 * chunks) + [jax.ShapeDtypeStruct((units, count), jnp.bfloat16)],
        in_specs=[anywhere] * (len(flat) + 3) + [in_vmem],
        out_specs=[in_vmem] * (2 * chunks + 1),
        scratch_shapes=[
            pltpu.VMEM((count, width), jnp.bfloat16),
            pltpu.VMEM((count, LANES), jnp.bfloat16),
            pltpu.VMEM((units, width), jnp.bfloat16),
            pltpu.VMEM((units, width), jnp.bfloat16),
            pltpu.VMEM((units, width), jnp.bfloat16),
            pltpu.SemaphoreType.DMA((8 * chunks + 11,)),
        ],
        compiler_params=pltpu.CompilerParams(vmem_limit_bytes=36 * MIB),
        cost_estimate=pl.CostEstimate(
            flops=6 * count * units * width,
            bytes_accessed=10 * count * width,
            transcendentals=count * units,
        ),
        name="expert_terms",
    )(*flat, gate_weight, up_weight, down_weight, sel)
    return outs[:-1], outs[-1]


def update_kernel(*refs):
    pieces = refs[:8]
    hidden_t_ref, down_ref, first_ref, second_ref = refs[8:12]
    new_down_ref, new_first_ref, new_second_ref = refs[-3:]
    cotangent = jnp.concatenate([piece[...] for piece in pieces], axis=0)
    gradient = jnp.dot(hidden_t_ref[...], cotangent, preferred_element_type=jnp.float32)
    new_down, new_first, new_second = adam_update(
        gradient, down_ref[...], first_ref[...], second_ref[...]
    )
    new_down_ref[...] = new_down
    new_first_ref[...] = new_first
    new_second_ref[...] = new_second


def update(pieces, hidden_t, down_weight, first_moment, second_moment, chunk, chunks, olds):
    units, width = down_weight.shape
    part = pieces[0].shape[0]
    block = 256
    steps = width // chunks // block
    state = pl.BlockSpec((units, block), lambda i: (0, i + chunk * steps))
    in_specs = [pl.BlockSpec((part, block), lambda i: (0, i))] * 8
    in_specs += [pl.BlockSpec(hidden_t.shape, lambda i: (0, 0))] + [state] * 3
    in_specs += [pl.BlockSpec(memory_space=pl.ANY)] * len(olds)
    return pl.pallas_call(
        update_kernel,
        grid=(steps,),
        out_shape=[jax.ShapeDtypeStruct((units, width), jnp.bfloat16)] * 3,
        in_specs=in_specs,
        out_specs=[state] * 3,
        input_output_aliases={12 + k: k for k in range(len(olds))},
        compiler_params=pltpu.CompilerParams(vmem_limit_bytes=24 * MIB),
        cost_estimate=pl.CostEstimate(
            flops=2 * 8 * part * units * width // chunks,
            bytes_accessed=14 * units * width // chunks,
            transcendentals=2 * units * width // chunks,
        ),
        name="update",
    )(*pieces, hidden_t, down_weight, first_moment, second_moment, *olds)


def dense_plan(
    tokens,
    expert_ids,
    gate_values,
    gate_weight,
    up_weight,
    down_weight,
    first_moment,
    second_moment,
):
    experts = lax.axis_size("expert")
    width = tokens.shape[1]
    span = width // CHUNKS
    hot_rows = experts * 3 // 4
    numbers = jnp.arange(LANES, dtype=jnp.int32)
    matches = (expert_ids[:, :, None] == numbers) & (numbers < experts)
    gates = jnp.sum(jnp.where(matches, gate_values[:, :, None], 0), axis=1)
    hot = jnp.any(expert_ids < experts, axis=1).astype(jnp.int32)
    rank = jnp.cumsum(hot) - hot
    place = jnp.arange(hot_rows, dtype=jnp.int32)
    pick = ((rank[None, :] == place[:, None]) & (hot[None, :] == 1)).astype(jnp.bfloat16)
    hot_tokens = jnp.dot(pick, tokens, preferred_element_type=jnp.float32).astype(jnp.bfloat16)
    hot_gates = jnp.dot(pick, gates, preferred_element_type=jnp.float32).astype(jnp.bfloat16)
    own = [hot_tokens[:, c * span : (c + 1) * span] for c in range(CHUNKS)]
    sent = [jnp.concatenate([own[0], hot_gates], axis=1)] + own[1:]
    pieces = [spread(block) for block in sent]
    sel = (numbers == lax.axis_index("expert")).astype(jnp.float32)[None, :]
    terms, hidden_t = expert_terms(pieces, gate_weight[0], up_weight[0], down_weight[0], sel)
    cotangents = []
    for c in range(CHUNKS):
        mixed = collect(terms[2 * c], terms[2 * c + 1])
        cotangents.append(
            spread(jnp.tanh(own[c].astype(jnp.float32) + mixed).astype(jnp.bfloat16))
        )
    outs = ()
    for c in range(CHUNKS):
        outs = update(
            cotangents[c],
            hidden_t,
            down_weight[0],
            first_moment[0],
            second_moment[0],
            c,
            CHUNKS,
            outs,
        )
    return tuple(out[None] for out in outs)


def solution(mesh):
    in_specs = (
        P(("dp", "expert"), None),
        P(("dp", "expert"), None),
        P(("dp", "expert"), None),
        P("expert", "dp", None),
        P("expert", "dp", None),
        P("expert", "dp", None),
        P("expert", "dp", None),
        P("expert", "dp", None),
    )
    out_specs = (P("expert", "dp", None), P("expert", "dp", None), P("expert", "dp", None))
    small = mesh.shape["dp"] == 2 and mesh.shape["expert"] == 16
    local = dense_plan if small else slot_plan
    return jax.shard_map(local, mesh=mesh, in_specs=in_specs, out_specs=out_specs, check_vma=False)
```

```python
import functools

import jax
import jax.numpy as jnp
from jax import lax
from jax.experimental import pallas as pl
from jax.experimental.pallas import tpu as pltpu
from jax.sharding import PartitionSpec as P

CAP = 6


first_decay = 0.9
second_decay = 0.95
learn_rate = 0.00024
weight_decay = 0.1
adam_epsilon = 1e-08
adam_count = 100.0


def slot_table(id_block, gate_block, experts, capacity):
    numbers = jnp.arange(experts, dtype=jnp.int32)
    matches = id_block[:, :, None] == numbers[None, None, :]
    member = jnp.sum(matches.astype(jnp.int32), axis=1)
    chosen = jnp.sum(
        jnp.where(matches, gate_block[:, :, None].astype(jnp.float32), jnp.float32(0.0)), axis=1
    )
    position = jnp.cumsum(member, axis=0) - member
    slot_ids = jnp.arange(capacity, dtype=jnp.int32)
    onehot = member[:, :, None] * (position[:, :, None] == slot_ids[None, None, :]).astype(
        jnp.int32
    )
    return (onehot, chosen)


def expert_hidden(expert_rows, gate_rows, up_rows):
    contract = (((1,), (1,)), ((), ()))
    gate_part = lax.dot_general(
        expert_rows, gate_rows, contract, preferred_element_type=jnp.float32
    )
    up_part = lax.dot_general(expert_rows, up_rows, contract, preferred_element_type=jnp.float32)
    return (jax.nn.silu(gate_part) * up_part).astype(jnp.bfloat16)


def adam_update(gradient, weight_rows, first_rows, second_rows):
    first_new = first_decay * first_rows.astype(jnp.float32) + (1.0 - first_decay) * gradient
    second_new = (
        second_decay * second_rows.astype(jnp.float32) + (1.0 - second_decay) * gradient * gradient
    )
    first_hat = first_new / (1.0 - first_decay**adam_count)
    second_hat = second_new / (1.0 - second_decay**adam_count)
    weight_new = weight_rows.astype(jnp.float32) * (
        1.0 - learn_rate * weight_decay
    ) - learn_rate * first_hat / (jnp.sqrt(second_hat) + adam_epsilon)
    return (
        weight_new.astype(jnp.bfloat16),
        first_new.astype(jnp.bfloat16),
        second_new.astype(jnp.bfloat16),
    )


def slot_plan(
    tokens,
    expert_ids,
    gate_values,
    gate_weight,
    up_weight,
    down_weight,
    first_moment,
    second_moment,
):
    experts = lax.axis_size("expert")
    tok_count, model_width = tokens.shape
    capacity = CAP
    slot_count = experts * capacity
    onehot, chosen = slot_table(expert_ids, gate_values, experts, capacity)
    dispatch_map = onehot.reshape(tok_count, slot_count).astype(jnp.bfloat16)
    combine_map = (
        (onehot.astype(jnp.float32) * chosen[:, :, None])
        .reshape(tok_count, slot_count)
        .astype(jnp.bfloat16)
    )
    over_tokens = (((0,), (0,)), ((), ()))
    outgoing = lax.dot_general(
        dispatch_map, tokens, over_tokens, preferred_element_type=jnp.float32
    ).astype(jnp.bfloat16)
    arrived = lax.all_to_all(
        outgoing.reshape(experts, capacity, model_width),
        "expert",
        split_axis=0,
        concat_axis=0,
        tiled=True,
    )
    arrived = arrived.reshape(slot_count, model_width)
    gate_full, up_full, down_full = (
        lax.all_gather(gate_weight, "dp", axis=1, tiled=True),
        lax.all_gather(up_weight, "dp", axis=1, tiled=True),
        lax.all_gather(down_weight, "dp", axis=1, tiled=True),
    )
    hidden = expert_hidden(arrived, gate_full[0], up_full[0])
    outputs = jnp.dot(hidden, down_full[0], preferred_element_type=jnp.float32).astype(jnp.bfloat16)
    returned = lax.all_to_all(
        outputs.reshape(experts, capacity, model_width),
        "expert",
        split_axis=0,
        concat_axis=0,
        tiled=True,
    )
    returned = returned.reshape(slot_count, model_width)
    mixed = jnp.dot(combine_map, returned, preferred_element_type=jnp.float32)
    cotangent = jnp.tanh(tokens.astype(jnp.float32) + mixed).astype(jnp.bfloat16)
    weighted = lax.dot_general(
        combine_map, cotangent, over_tokens, preferred_element_type=jnp.float32
    ).astype(jnp.bfloat16)
    arrived_grad = lax.all_to_all(
        weighted.reshape(experts, capacity, model_width),
        "expert",
        split_axis=0,
        concat_axis=0,
        tiled=True,
    )
    arrived_grad = arrived_grad.reshape(slot_count, model_width)
    gradient = lax.psum_scatter(
        lax.dot_general(
            hidden, arrived_grad, over_tokens, preferred_element_type=jnp.float32
        ).astype(jnp.bfloat16),
        "dp",
        scatter_dimension=0,
        tiled=True,
    ).astype(jnp.float32)
    new_down, new_first, new_second = adam_update(
        gradient, down_weight[0], first_moment[0], second_moment[0]
    )
    return (new_down[None], new_first[None], new_second[None])


AXES = ("dp", "expert")
CORE = 1
PLANE = (2, 16, 18)
LINE = (4, 8, 12)
BLOCK = 512
PARTS = 2
LIMIT = 48
LANES = 128
MIB = 1024 * 1024


def swap(block, mask):
    count = lax.axis_size(AXES)
    return lax.ppermute(block, AXES, [(i, i ^ mask) for i in range(count)])


def spread(block):
    block = jnp.concatenate([block] + [swap(block, mask) for mask in LINE], axis=0)
    return [block] + [swap(block, mask) for mask in PLANE]


def to_core(pieces):
    return [swap(piece, CORE) for piece in pieces]


def add_parts(own, other_parts):
    total = own.astype(jnp.float32)
    for part in other_parts:
        total = total + part.astype(jnp.float32)
    return total


def collect(own, other):
    total = add_parts(own, [swap(other, CORE)])
    for masks in (PLANE, LINE):
        parts = jnp.split(total, len(masks) + 1, axis=0)
        sent = [swap(part.astype(jnp.bfloat16), mask) for part, mask in zip(parts[1:], masks)]
        total = add_parts(parts[0], sent)
    return total


def expert_kernel(*refs):
    pieces = refs[:8]
    gate_ref, up_ref, down_ref, own_ref, other_ref, hidden_t_ref = refs[8:14]
    gate_vm, up_vm, down_vm, rows, sems = refs[14:]
    count, width = rows.shape
    part = count // 8
    spans = [pl.ds(start, width // PARTS) for start in range(0, width, width // PARTS)]
    loads = [
        [
            pltpu.make_async_copy(src.at[:, span], dst.at[:, span], sems.at[PARTS * k + s])
            for s, span in enumerate(spans)
        ]
        for k, (src, dst) in enumerate(
            ((gate_ref, gate_vm), (up_ref, up_vm), (down_ref, down_vm))
        )
    ]
    for s in range(PARTS):
        loads[0][s].start()
        loads[1][s].start()
    for load in loads[2]:
        load.start()
    for p in range(8):
        rows[p * part : (p + 1) * part] = pieces[p][:, :width]
    gates = jnp.concatenate([piece[:, width:] for piece in pieces], axis=0).astype(jnp.float32)
    lane = lax.broadcasted_iota(jnp.int32, gates.shape, 1)
    gates = jnp.where(lane == lax.axis_index("expert"), gates, 0.0)
    gate = jnp.sum(gates, axis=1, keepdims=True)
    contract = (((1,), (1,)), ((), ()))
    gate_part, up_part = 0.0, 0.0
    for s, span in enumerate(spans):
        loads[0][s].wait()
        gate_part += lax.dot_general(
            rows[:, span], gate_vm[:, span], contract, preferred_element_type=jnp.float32
        )
        loads[1][s].wait()
        up_part += lax.dot_general(
            rows[:, span], up_vm[:, span], contract, preferred_element_type=jnp.float32
        )
    hidden = gate * (jax.nn.silu(gate_part) * up_part)
    hidden_t_ref[...] = hidden.T.astype(jnp.bfloat16)
    hidden = hidden.astype(jnp.bfloat16)
    for load, span in zip(loads[2], spans):
        load.wait()
        terms = jnp.dot(hidden, down_vm[:, span], preferred_element_type=jnp.float32)
        terms = terms.astype(jnp.bfloat16)
        own_ref[:, span] = terms[: count // 2]
        other_ref[:, span] = terms[count // 2 :]


def expert_terms(pieces, gate_weight, up_weight, down_weight):
    units, width = gate_weight.shape
    count = 8 * pieces[0].shape[0]
    half = jax.ShapeDtypeStruct((count // 2, width), jnp.bfloat16)
    in_vmem = pl.BlockSpec(memory_space=pltpu.VMEM)
    in_hbm = pl.BlockSpec(memory_space=pltpu.HBM)
    return pl.pallas_call(
        expert_kernel,
        out_shape=[half, half, jax.ShapeDtypeStruct((units, count), jnp.bfloat16)],
        in_specs=[in_vmem] * 8 + [in_hbm] * 3,
        out_specs=[in_vmem] * 3,
        scratch_shapes=[pltpu.VMEM((units, width), jnp.bfloat16)] * 3
        + [pltpu.VMEM((count, width), jnp.bfloat16), pltpu.SemaphoreType.DMA((3 * PARTS,))],
        compiler_params=pltpu.CompilerParams(vmem_limit_bytes=LIMIT * MIB),
        cost_estimate=pl.CostEstimate(
            flops=6 * count * units * width,
            bytes_accessed=10 * count * width,
            transcendentals=count * units,
        ),
        name="expert_terms",
    )(*pieces, gate_weight, up_weight, down_weight)


def update_kernel(block, *refs):
    pieces = refs[:8]
    hidden_t_ref, down_ref, first_ref, second_ref = refs[8:12]
    new_down_ref, new_first_ref, new_second_ref = refs[12:]
    span = pl.ds(pl.multiple_of(pl.program_id(0) * block, LANES), block)
    cotangent = jnp.concatenate([piece[:, span] for piece in pieces], axis=0)
    gradient = jnp.dot(hidden_t_ref[...], cotangent, preferred_element_type=jnp.float32)
    first = first_decay * first_ref[:, span].astype(jnp.float32) + (1.0 - first_decay) * gradient
    second = (
        second_decay * second_ref[:, span].astype(jnp.float32)
        + (1.0 - second_decay) * gradient * gradient
    )
    root = (1.0 - second_decay**adam_count) ** 0.5
    rate = learn_rate * root / (1.0 - first_decay**adam_count)
    keep = 1.0 - learn_rate * weight_decay
    step = rate * first / (jnp.sqrt(second) + adam_epsilon * root)
    new_down_ref[...] = (keep * down_ref[:, span].astype(jnp.float32) - step).astype(jnp.bfloat16)
    new_first_ref[...] = first.astype(jnp.bfloat16)
    new_second_ref[...] = second.astype(jnp.bfloat16)


def update(pieces, hidden_t, down_weight, first_moment, second_moment):
    units, width = down_weight.shape
    part = pieces[0].shape[0]
    in_vmem = pl.BlockSpec(memory_space=pltpu.VMEM)
    return pl.pallas_call(
        functools.partial(update_kernel, BLOCK),
        grid=(width // BLOCK,),
        out_shape=[jax.ShapeDtypeStruct((units, width), jnp.bfloat16)] * 3,
        in_specs=[in_vmem] * 12,
        out_specs=[pl.BlockSpec((units, BLOCK), lambda i: (0, i))] * 3,
        compiler_params=pltpu.CompilerParams(vmem_limit_bytes=24 * MIB),
        cost_estimate=pl.CostEstimate(
            flops=2 * 8 * part * units * width,
            bytes_accessed=14 * units * width,
            transcendentals=2 * units * width,
        ),
        name="update",
    )(*pieces, hidden_t, down_weight, first_moment, second_moment)


def dense_plan(
    tokens,
    expert_ids,
    gate_values,
    gate_weight,
    up_weight,
    down_weight,
    first_moment,
    second_moment,
):
    experts = lax.axis_size("expert")
    hot_rows = experts * 3 // 4
    numbers = jnp.arange(LANES, dtype=jnp.int32)
    matches = (expert_ids[:, :, None] == numbers) & (numbers < experts)
    gates = jnp.sum(jnp.where(matches, gate_values[:, :, None], 0), axis=1)
    hot = jnp.any(expert_ids < experts, axis=1).astype(jnp.int32)
    rank = jnp.cumsum(hot) - hot
    place = jnp.arange(hot_rows, dtype=jnp.int32)
    pick = ((rank[None, :] == place[:, None]) & (hot[None, :] == 1)).astype(jnp.bfloat16)
    hot_tokens = jnp.dot(pick, tokens, preferred_element_type=jnp.float32).astype(jnp.bfloat16)
    hot_gates = jnp.dot(pick, gates, preferred_element_type=jnp.float32).astype(jnp.bfloat16)
    pieces = spread(jnp.concatenate([hot_tokens, hot_gates], axis=1))
    pieces += to_core(pieces)
    own, other, hidden_t = expert_terms(pieces, gate_weight[0], up_weight[0], down_weight[0])
    mixed = collect(own, other)
    cotangent = jnp.tanh(hot_tokens.astype(jnp.float32) + mixed).astype(jnp.bfloat16)
    pieces = spread(cotangent)
    pieces += to_core(pieces)
    outs = update(pieces, hidden_t, down_weight[0], first_moment[0], second_moment[0])
    return tuple(out[None] for out in outs)


def solution(mesh):
    in_specs = (
        P(("dp", "expert"), None),
        P(("dp", "expert"), None),
        P(("dp", "expert"), None),
        P("expert", "dp", None),
        P("expert", "dp", None),
        P("expert", "dp", None),
        P("expert", "dp", None),
        P("expert", "dp", None),
    )
    out_specs = (P("expert", "dp", None), P("expert", "dp", None), P("expert", "dp", None))
    small = mesh.shape["dp"] == 2 and mesh.shape["expert"] == 16
    local = dense_plan if small else slot_plan
    return jax.shard_map(local, mesh=mesh, in_specs=in_specs, out_specs=out_specs, check_vma=False)
```

```python
import functools

import jax
import jax.numpy as jnp
from jax import lax
from jax.experimental import pallas as pl
from jax.experimental.pallas import tpu as pltpu
from jax.sharding import PartitionSpec as P

CAP = 6


first_decay = 0.9
second_decay = 0.95
learn_rate = 0.00024
weight_decay = 0.1
adam_epsilon = 1e-08
adam_count = 100.0


def slot_table(id_block, gate_block, experts, capacity):
    numbers = jnp.arange(experts, dtype=jnp.int32)
    matches = id_block[:, :, None] == numbers[None, None, :]
    member = jnp.sum(matches.astype(jnp.int32), axis=1)
    chosen = jnp.sum(
        jnp.where(matches, gate_block[:, :, None].astype(jnp.float32), jnp.float32(0.0)), axis=1
    )
    position = jnp.cumsum(member, axis=0) - member
    slot_ids = jnp.arange(capacity, dtype=jnp.int32)
    onehot = member[:, :, None] * (position[:, :, None] == slot_ids[None, None, :]).astype(
        jnp.int32
    )
    return (onehot, chosen)


def expert_hidden(expert_rows, gate_rows, up_rows):
    contract = (((1,), (1,)), ((), ()))
    gate_part = lax.dot_general(
        expert_rows, gate_rows, contract, preferred_element_type=jnp.float32
    )
    up_part = lax.dot_general(expert_rows, up_rows, contract, preferred_element_type=jnp.float32)
    return (jax.nn.silu(gate_part) * up_part).astype(jnp.bfloat16)


def adam_update(gradient, weight_rows, first_rows, second_rows):
    first_new = first_decay * first_rows.astype(jnp.float32) + (1.0 - first_decay) * gradient
    second_new = (
        second_decay * second_rows.astype(jnp.float32) + (1.0 - second_decay) * gradient * gradient
    )
    first_hat = first_new / (1.0 - first_decay**adam_count)
    second_hat = second_new / (1.0 - second_decay**adam_count)
    weight_new = weight_rows.astype(jnp.float32) * (
        1.0 - learn_rate * weight_decay
    ) - learn_rate * first_hat / (jnp.sqrt(second_hat) + adam_epsilon)
    return (
        weight_new.astype(jnp.bfloat16),
        first_new.astype(jnp.bfloat16),
        second_new.astype(jnp.bfloat16),
    )


def slot_plan(
    tokens,
    expert_ids,
    gate_values,
    gate_weight,
    up_weight,
    down_weight,
    first_moment,
    second_moment,
):
    experts = lax.axis_size("expert")
    tok_count, model_width = tokens.shape
    capacity = CAP
    slot_count = experts * capacity
    onehot, chosen = slot_table(expert_ids, gate_values, experts, capacity)
    dispatch_map = onehot.reshape(tok_count, slot_count).astype(jnp.bfloat16)
    combine_map = (
        (onehot.astype(jnp.float32) * chosen[:, :, None])
        .reshape(tok_count, slot_count)
        .astype(jnp.bfloat16)
    )
    over_tokens = (((0,), (0,)), ((), ()))
    outgoing = lax.dot_general(
        dispatch_map, tokens, over_tokens, preferred_element_type=jnp.float32
    ).astype(jnp.bfloat16)
    arrived = lax.all_to_all(
        outgoing.reshape(experts, capacity, model_width),
        "expert",
        split_axis=0,
        concat_axis=0,
        tiled=True,
    )
    arrived = arrived.reshape(slot_count, model_width)
    gate_full, up_full, down_full = (
        lax.all_gather(gate_weight, "dp", axis=1, tiled=True),
        lax.all_gather(up_weight, "dp", axis=1, tiled=True),
        lax.all_gather(down_weight, "dp", axis=1, tiled=True),
    )
    hidden = expert_hidden(arrived, gate_full[0], up_full[0])
    outputs = jnp.dot(hidden, down_full[0], preferred_element_type=jnp.float32).astype(jnp.bfloat16)
    returned = lax.all_to_all(
        outputs.reshape(experts, capacity, model_width),
        "expert",
        split_axis=0,
        concat_axis=0,
        tiled=True,
    )
    returned = returned.reshape(slot_count, model_width)
    mixed = jnp.dot(combine_map, returned, preferred_element_type=jnp.float32)
    cotangent = jnp.tanh(tokens.astype(jnp.float32) + mixed).astype(jnp.bfloat16)
    weighted = lax.dot_general(
        combine_map, cotangent, over_tokens, preferred_element_type=jnp.float32
    ).astype(jnp.bfloat16)
    arrived_grad = lax.all_to_all(
        weighted.reshape(experts, capacity, model_width),
        "expert",
        split_axis=0,
        concat_axis=0,
        tiled=True,
    )
    arrived_grad = arrived_grad.reshape(slot_count, model_width)
    gradient = lax.psum_scatter(
        lax.dot_general(
            hidden, arrived_grad, over_tokens, preferred_element_type=jnp.float32
        ).astype(jnp.bfloat16),
        "dp",
        scatter_dimension=0,
        tiled=True,
    ).astype(jnp.float32)
    new_down, new_first, new_second = adam_update(
        gradient, down_weight[0], first_moment[0], second_moment[0]
    )
    return (new_down[None], new_first[None], new_second[None])


AXES = ("dp", "expert")
CORE = 1
PLANE = (2, 16, 18)
LINE = (8, 4, 12)
BLOCK = 512
UPDATE_BLOCK = 256
PARTS = 4
LIMIT = 48
PACK_PARTS = 4
PACK_LIMIT = 60
LANES = 128
MIB = 1024 * 1024


def swap(block, mask):
    count = lax.axis_size(AXES)
    return lax.ppermute(block, AXES, [(i, i ^ mask) for i in range(count)])


def spread(block):
    block = jnp.concatenate([block] + [swap(block, mask) for mask in LINE], axis=0)
    return across(block)


def across(block):
    return [block] + [swap(block, mask) for mask in PLANE]


def to_core(pieces):
    return [swap(piece, CORE) for piece in pieces]


def add_parts(own, other_parts):
    total = own.astype(jnp.float32)
    for part in other_parts:
        total = total + part.astype(jnp.float32)
    return total


def collect(own, other):
    total = add_parts(own, [swap(other, CORE)])
    parts = jnp.split(total, len(PLANE) + 1, axis=0)
    sent = [swap(part.astype(jnp.bfloat16), mask) for part, mask in zip(parts[1:], PLANE)]
    kept, sent = jnp.split(add_parts(parts[0], sent), 2, axis=0)
    pair = add_parts(kept, [swap(sent.astype(jnp.bfloat16), LINE[1])]).astype(jnp.bfloat16)
    mine, its = jnp.split(pair, 2, axis=0)
    return add_parts(pair, [swap(jnp.concatenate([its, mine], axis=0), LINE[0])])


def pack_kernel(experts, tokens_ref, ids_ref, gates_ref, out_ref, *scratch):
    tokens_vm, ids_vm, gates_vm, sems = scratch
    count, width = tokens_vm.shape
    part = count // PACK_PARTS
    loads = [
        pltpu.make_async_copy(
            tokens_ref.at[pl.ds(k * part, part)], tokens_vm.at[pl.ds(k * part, part)], sems.at[k]
        )
        for k in range(PACK_PARTS)
    ]
    ids_load = pltpu.make_async_copy(ids_ref, ids_vm, sems.at[PACK_PARTS])
    gates_load = pltpu.make_async_copy(gates_ref, gates_vm, sems.at[PACK_PARTS + 1])
    for load in [ids_load, gates_load] + loads:
        load.start()
    ids_load.wait()
    gates_load.wait()
    ids, values = ids_vm[...], gates_vm[...].astype(jnp.float32)
    row = lax.broadcasted_iota(jnp.int32, (LANES, count), 0)
    gates = jnp.zeros((LANES, count), jnp.float32)
    hot = jnp.zeros((LANES, count), jnp.bool_)
    for k in range(ids.shape[0]):
        named = jnp.broadcast_to(ids[k : k + 1], row.shape)
        gates += jnp.where((named == row) & (row < experts), values[k : k + 1], 0.0)
        hot |= named < experts
    source = lax.broadcasted_iota(jnp.int32, (count, count), 0)
    target = lax.broadcasted_iota(jnp.int32, (count, count), 1)
    before = jnp.where(source < target, 1.0, 0.0).astype(jnp.bfloat16)
    marks = jnp.where(hot, 1.0, 0.0).astype(jnp.bfloat16)
    rank = jnp.dot(marks, before, preferred_element_type=jnp.float32)
    pick = jnp.where(hot & (rank.astype(jnp.int32) == row), 1.0, 0.0).astype(jnp.bfloat16)
    rows = out_ref.shape[0]
    pick = pick[: 16 * pl.cdiv(rows, 16)]
    hot_gates = lax.dot_general(
        pick,
        gates.astype(jnp.bfloat16),
        (((1,), (1,)), ((), ())),
        preferred_element_type=jnp.float32,
    )
    out_ref[:, width:] = hot_gates[:rows].astype(jnp.bfloat16)
    for load in loads:
        load.wait()
    hot_tokens = jnp.dot(pick, tokens_vm[...], preferred_element_type=jnp.float32)
    out_ref[:, :width] = hot_tokens[:rows].astype(jnp.bfloat16)


def pack(tokens, expert_ids, gate_values, experts):
    in_vmem = pl.BlockSpec(memory_space=pltpu.VMEM)
    return pl.pallas_call(
        functools.partial(pack_kernel, experts),
        out_shape=jax.ShapeDtypeStruct((experts * 3 // 4, tokens.shape[1] + LANES), jnp.bfloat16),
        in_specs=[pl.BlockSpec(memory_space=pltpu.HBM)] * 3,
        out_specs=in_vmem,
        scratch_shapes=[
            pltpu.VMEM(tokens.shape, tokens.dtype),
            pltpu.VMEM(expert_ids.shape[::-1], expert_ids.dtype),
            pltpu.VMEM(gate_values.shape[::-1], gate_values.dtype),
            pltpu.SemaphoreType.DMA((PACK_PARTS + 2,)),
        ],
        compiler_params=pltpu.CompilerParams(vmem_limit_bytes=PACK_LIMIT * MIB),
        name="pack",
    )(tokens, expert_ids.T, gate_values.T)


def expert_kernel(*refs):
    pieces = refs[:8]
    gate_ref, up_ref, down_ref, own_ref, other_ref, hidden_t_ref = refs[8:14]
    gate_vm, up_vm, down_vm, rows, sems = refs[14:]
    count, width = rows.shape
    part = count // 8
    units = gate_vm.shape[0]
    loads = [
        [
            pltpu.make_async_copy(
                src.at[pl.ds(s * units // PARTS, units // PARTS)],
                dst.at[pl.ds(s * units // PARTS, units // PARTS)],
                sems.at[PARTS * k + s],
            )
            for s in range(PARTS)
        ]
        for k, (src, dst) in enumerate(
            ((gate_ref, gate_vm), (up_ref, up_vm), (down_ref, down_vm))
        )
    ]
    for weight in loads:
        for load in weight:
            load.start()
    for p in range(8):
        rows[p * part : (p + 1) * part] = pieces[p][:, :width]
    gates = jnp.concatenate([piece[:, width:] for piece in pieces], axis=0).astype(jnp.float32)
    lane = lax.broadcasted_iota(jnp.int32, gates.shape, 1)
    gates = jnp.where(lane == lax.axis_index("expert"), gates, 0.0)
    gate = jnp.sum(gates, axis=1, keepdims=True)
    contract = (((1,), (1,)), ((), ()))
    for load in loads[0]:
        load.wait()
    gate_part = lax.dot_general(
        rows[...], gate_vm[...], contract, preferred_element_type=jnp.float32
    )
    for load in loads[1]:
        load.wait()
    up_part = lax.dot_general(rows[...], up_vm[...], contract, preferred_element_type=jnp.float32)
    hidden = gate * (jax.nn.silu(gate_part) * up_part)
    hidden_t_ref[...] = hidden.T.astype(jnp.bfloat16)
    hidden = hidden.astype(jnp.bfloat16)
    for load in loads[2]:
        load.wait()
    for start in range(0, width, BLOCK):
        span = slice(start, start + BLOCK)
        terms = jnp.dot(hidden, down_vm[:, span], preferred_element_type=jnp.float32)
        terms = terms.astype(jnp.bfloat16)
        own_ref[:, span] = terms[: count // 2]
        other_ref[:, span] = terms[count // 2 :]


def expert_terms(pieces, gate_weight, up_weight, down_weight):
    units, width = gate_weight.shape
    count = 8 * pieces[0].shape[0]
    half = jax.ShapeDtypeStruct((count // 2, width), jnp.bfloat16)
    in_vmem = pl.BlockSpec(memory_space=pltpu.VMEM)
    in_hbm = pl.BlockSpec(memory_space=pltpu.HBM)
    return pl.pallas_call(
        expert_kernel,
        out_shape=[half, half, jax.ShapeDtypeStruct((units, count), jnp.bfloat16)],
        in_specs=[in_vmem] * 8 + [in_hbm] * 3,
        out_specs=[in_vmem] * 3,
        scratch_shapes=[pltpu.VMEM((units, width), jnp.bfloat16)] * 3
        + [pltpu.VMEM((count, width), jnp.bfloat16), pltpu.SemaphoreType.DMA((3 * PARTS,))],
        compiler_params=pltpu.CompilerParams(vmem_limit_bytes=LIMIT * MIB),
        cost_estimate=pl.CostEstimate(
            flops=6 * count * units * width,
            bytes_accessed=10 * count * width,
            transcendentals=count * units,
        ),
        name="expert_terms",
    )(*pieces, gate_weight, up_weight, down_weight)


def update_kernel(*refs):
    pieces = refs[:8]
    hidden_t_ref, down_ref, first_ref, second_ref = refs[8:12]
    outs, held, sems = refs[12:15], refs[15:18], refs[18]
    root = (1.0 - second_decay**adam_count) ** 0.5
    rate = learn_rate * root / (1.0 - first_decay**adam_count)
    keep = 1.0 - learn_rate * weight_decay
    stores = []
    for start in range(0, down_ref.shape[1], UPDATE_BLOCK):
        span = pl.ds(start, UPDATE_BLOCK)
        cotangent = jnp.concatenate([piece[:, span] for piece in pieces], axis=0)
        gradient = jnp.dot(hidden_t_ref[...], cotangent, preferred_element_type=jnp.float32)
        first = first_decay * first_ref[:, span].astype(jnp.float32)
        first += (1.0 - first_decay) * gradient
        second = second_decay * second_ref[:, span].astype(jnp.float32)
        second += (1.0 - second_decay) * gradient * gradient
        step = rate * first / (jnp.sqrt(second) + adam_epsilon * root)
        down = keep * down_ref[:, span].astype(jnp.float32) - step
        for k, value in enumerate((down, first, second)):
            held[k][:, span] = value.astype(jnp.bfloat16)
            stores.append(
                pltpu.make_async_copy(
                    held[k].at[:, span], outs[k].at[:, span], sems.at[len(stores)]
                )
            )
            stores[-1].start()
    for store in stores:
        store.wait()


def update(pieces, hidden_t, down_weight, first_moment, second_moment):
    units, width = down_weight.shape
    part = pieces[0].shape[0]
    return pl.pallas_call(
        update_kernel,
        out_shape=[jax.ShapeDtypeStruct((units, width), jnp.bfloat16)] * 3,
        in_specs=[pl.BlockSpec(memory_space=pltpu.VMEM)] * 12,
        out_specs=[pl.BlockSpec(memory_space=pltpu.HBM)] * 3,
        scratch_shapes=[pltpu.VMEM((units, width), jnp.bfloat16)] * 3
        + [pltpu.SemaphoreType.DMA((3 * width // UPDATE_BLOCK,))],
        compiler_params=pltpu.CompilerParams(vmem_limit_bytes=24 * MIB),
        cost_estimate=pl.CostEstimate(
            flops=2 * 8 * part * units * width,
            bytes_accessed=14 * units * width,
            transcendentals=2 * units * width,
        ),
        name="update",
    )(*pieces, hidden_t, down_weight, first_moment, second_moment)


def dense_plan(
    tokens,
    expert_ids,
    gate_values,
    gate_weight,
    up_weight,
    down_weight,
    first_moment,
    second_moment,
):
    experts = lax.axis_size("expert")
    width = tokens.shape[1]
    pieces = spread(pack(tokens, expert_ids, gate_values, experts))
    pair_tokens = pieces[0][: 2 * (experts * 3 // 4), :width].astype(jnp.float32)
    pieces += to_core(pieces)
    own, other, hidden_t = expert_terms(pieces, gate_weight[0], up_weight[0], down_weight[0])
    cotangent = jnp.tanh(pair_tokens + collect(own, other)).astype(jnp.bfloat16)
    cotangent = jnp.concatenate([cotangent, swap(cotangent, LINE[1])], axis=0)
    pieces = across(cotangent)
    pieces += to_core(pieces)
    outs = update(pieces, hidden_t, down_weight[0], first_moment[0], second_moment[0])
    return tuple(out[None] for out in outs)


def solution(mesh):
    in_specs = (
        P(("dp", "expert"), None),
        P(("dp", "expert"), None),
        P(("dp", "expert"), None),
        P("expert", "dp", None),
        P("expert", "dp", None),
        P("expert", "dp", None),
        P("expert", "dp", None),
        P("expert", "dp", None),
    )
    out_specs = (P("expert", "dp", None), P("expert", "dp", None), P("expert", "dp", None))
    small = mesh.shape["dp"] == 2 and mesh.shape["expert"] == 16
    local = dense_plan if small else slot_plan
    return jax.shard_map(local, mesh=mesh, in_specs=in_specs, out_specs=out_specs, check_vma=False)
```

```python
import functools

import jax
import jax.numpy as jnp
from jax import lax
from jax.experimental import pallas as pl
from jax.experimental.pallas import tpu as pltpu
from jax.sharding import PartitionSpec as P

CAP = 6


first_decay = 0.9
second_decay = 0.95
learn_rate = 0.00024
weight_decay = 0.1
adam_epsilon = 1e-08
adam_count = 100.0


def slot_table(id_block, gate_block, experts, capacity):
    numbers = jnp.arange(experts, dtype=jnp.int32)
    matches = id_block[:, :, None] == numbers[None, None, :]
    member = jnp.sum(matches.astype(jnp.int32), axis=1)
    chosen = jnp.sum(
        jnp.where(matches, gate_block[:, :, None].astype(jnp.float32), jnp.float32(0.0)), axis=1
    )
    position = jnp.cumsum(member, axis=0) - member
    slot_ids = jnp.arange(capacity, dtype=jnp.int32)
    onehot = member[:, :, None] * (position[:, :, None] == slot_ids[None, None, :]).astype(
        jnp.int32
    )
    return (onehot, chosen)


def expert_hidden(expert_rows, gate_rows, up_rows):
    contract = (((1,), (1,)), ((), ()))
    gate_part = lax.dot_general(
        expert_rows, gate_rows, contract, preferred_element_type=jnp.float32
    )
    up_part = lax.dot_general(expert_rows, up_rows, contract, preferred_element_type=jnp.float32)
    return (jax.nn.silu(gate_part) * up_part).astype(jnp.bfloat16)


def adam_update(gradient, weight_rows, first_rows, second_rows):
    first_new = first_decay * first_rows.astype(jnp.float32) + (1.0 - first_decay) * gradient
    second_new = (
        second_decay * second_rows.astype(jnp.float32) + (1.0 - second_decay) * gradient * gradient
    )
    first_hat = first_new / (1.0 - first_decay**adam_count)
    second_hat = second_new / (1.0 - second_decay**adam_count)
    weight_new = weight_rows.astype(jnp.float32) * (
        1.0 - learn_rate * weight_decay
    ) - learn_rate * first_hat / (jnp.sqrt(second_hat) + adam_epsilon)
    return (
        weight_new.astype(jnp.bfloat16),
        first_new.astype(jnp.bfloat16),
        second_new.astype(jnp.bfloat16),
    )


def slot_plan(
    tokens,
    expert_ids,
    gate_values,
    gate_weight,
    up_weight,
    down_weight,
    first_moment,
    second_moment,
):
    experts = lax.axis_size("expert")
    tok_count, model_width = tokens.shape
    capacity = CAP
    slot_count = experts * capacity
    onehot, chosen = slot_table(expert_ids, gate_values, experts, capacity)
    dispatch_map = onehot.reshape(tok_count, slot_count).astype(jnp.bfloat16)
    combine_map = (
        (onehot.astype(jnp.float32) * chosen[:, :, None])
        .reshape(tok_count, slot_count)
        .astype(jnp.bfloat16)
    )
    over_tokens = (((0,), (0,)), ((), ()))
    outgoing = lax.dot_general(
        dispatch_map, tokens, over_tokens, preferred_element_type=jnp.float32
    ).astype(jnp.bfloat16)
    arrived = lax.all_to_all(
        outgoing.reshape(experts, capacity, model_width),
        "expert",
        split_axis=0,
        concat_axis=0,
        tiled=True,
    )
    arrived = arrived.reshape(slot_count, model_width)
    gate_full, up_full, down_full = (
        lax.all_gather(gate_weight, "dp", axis=1, tiled=True),
        lax.all_gather(up_weight, "dp", axis=1, tiled=True),
        lax.all_gather(down_weight, "dp", axis=1, tiled=True),
    )
    hidden = expert_hidden(arrived, gate_full[0], up_full[0])
    outputs = jnp.dot(hidden, down_full[0], preferred_element_type=jnp.float32).astype(jnp.bfloat16)
    returned = lax.all_to_all(
        outputs.reshape(experts, capacity, model_width),
        "expert",
        split_axis=0,
        concat_axis=0,
        tiled=True,
    )
    returned = returned.reshape(slot_count, model_width)
    mixed = jnp.dot(combine_map, returned, preferred_element_type=jnp.float32)
    cotangent = jnp.tanh(tokens.astype(jnp.float32) + mixed).astype(jnp.bfloat16)
    weighted = lax.dot_general(
        combine_map, cotangent, over_tokens, preferred_element_type=jnp.float32
    ).astype(jnp.bfloat16)
    arrived_grad = lax.all_to_all(
        weighted.reshape(experts, capacity, model_width),
        "expert",
        split_axis=0,
        concat_axis=0,
        tiled=True,
    )
    arrived_grad = arrived_grad.reshape(slot_count, model_width)
    gradient = lax.psum_scatter(
        lax.dot_general(
            hidden, arrived_grad, over_tokens, preferred_element_type=jnp.float32
        ).astype(jnp.bfloat16),
        "dp",
        scatter_dimension=0,
        tiled=True,
    ).astype(jnp.float32)
    new_down, new_first, new_second = adam_update(
        gradient, down_weight[0], first_moment[0], second_moment[0]
    )
    return (new_down[None], new_first[None], new_second[None])


AXES = ("dp", "expert")
CORE = 1
PLANE = (2, 16, 18)
LINE = (8, 4, 12)
BLOCK = 512
UPDATE_BLOCK = 256
PARTS = 4
LIMIT = 46
PACK_PARTS = 4
PACK_LIMIT = 60
LANES = 128
MIB = 1024 * 1024


def swap(block, mask):
    count = lax.axis_size(AXES)
    return lax.ppermute(block, AXES, [(i, i ^ mask) for i in range(count)])


def spread(block):
    block = jnp.concatenate([block] + [swap(block, mask) for mask in LINE], axis=0)
    return across(block)


def across(block):
    return [block] + [swap(block, mask) for mask in PLANE]


def to_core(pieces):
    return [swap(piece, CORE) for piece in pieces]


def add_parts(own, other_parts):
    total = own.astype(jnp.float32)
    for part in other_parts:
        total = total + part.astype(jnp.float32)
    return total


def collect(own, other):
    total = add_parts(own, [swap(other, CORE)])
    own, first, second, both = jnp.split(total, len(PLANE) + 1, axis=0)
    half = total.shape[1] // 2
    low = swap(both[:, :half].astype(jnp.bfloat16), PLANE[0])
    high = swap(both[:, half:].astype(jnp.bfloat16), PLANE[1])
    first = jnp.concatenate([first[:, :half], add_parts(first[:, half:], [high])], axis=1)
    second = jnp.concatenate([add_parts(second[:, :half], [low]), second[:, half:]], axis=1)
    sent = [swap(first.astype(jnp.bfloat16), PLANE[0]), swap(second.astype(jnp.bfloat16), PLANE[1])]
    kept, sent = jnp.split(add_parts(own, sent), 2, axis=0)
    pair = add_parts(kept, [swap(sent.astype(jnp.bfloat16), LINE[1])]).astype(jnp.bfloat16)
    mine, its = jnp.split(pair, 2, axis=0)
    return add_parts(pair, [swap(jnp.concatenate([its, mine], axis=0), LINE[0])])


def pack_kernel(experts, tokens_ref, ids_ref, gates_ref, out_ref, *scratch):
    tokens_vm, ids_vm, gates_vm, sems = scratch
    count, width = tokens_vm.shape
    part = count // PACK_PARTS
    loads = [
        pltpu.make_async_copy(
            tokens_ref.at[pl.ds(k * part, part)], tokens_vm.at[pl.ds(k * part, part)], sems.at[k]
        )
        for k in range(PACK_PARTS)
    ]
    ids_load = pltpu.make_async_copy(ids_ref, ids_vm, sems.at[PACK_PARTS])
    gates_load = pltpu.make_async_copy(gates_ref, gates_vm, sems.at[PACK_PARTS + 1])
    for load in [ids_load, gates_load] + loads:
        load.start()
    ids_load.wait()
    gates_load.wait()
    ids, values = ids_vm[...], gates_vm[...].astype(jnp.float32)
    row = lax.broadcasted_iota(jnp.int32, (LANES, count), 0)
    gates = jnp.zeros((LANES, count), jnp.float32)
    hot = jnp.zeros((LANES, count), jnp.bool_)
    for k in range(ids.shape[0]):
        named = jnp.broadcast_to(ids[k : k + 1], row.shape)
        gates += jnp.where((named == row) & (row < experts), values[k : k + 1], 0.0)
        hot |= named < experts
    source = lax.broadcasted_iota(jnp.int32, (count, count), 0)
    target = lax.broadcasted_iota(jnp.int32, (count, count), 1)
    before = jnp.where(source < target, 1.0, 0.0).astype(jnp.bfloat16)
    marks = jnp.where(hot, 1.0, 0.0).astype(jnp.bfloat16)
    rank = jnp.dot(marks, before, preferred_element_type=jnp.float32)
    pick = jnp.where(hot & (rank.astype(jnp.int32) == row), 1.0, 0.0).astype(jnp.bfloat16)
    rows = out_ref.shape[0]
    pick = pick[: 16 * pl.cdiv(rows, 16)]
    hot_gates = lax.dot_general(
        pick,
        gates.astype(jnp.bfloat16),
        (((1,), (1,)), ((), ())),
        preferred_element_type=jnp.float32,
    )
    out_ref[:, width:] = hot_gates[:rows].astype(jnp.bfloat16)
    for load in loads:
        load.wait()
    hot_tokens = jnp.dot(pick, tokens_vm[...], preferred_element_type=jnp.float32)
    out_ref[:, :width] = hot_tokens[:rows].astype(jnp.bfloat16)


def pack(tokens, expert_ids, gate_values, experts):
    in_vmem = pl.BlockSpec(memory_space=pltpu.VMEM)
    return pl.pallas_call(
        functools.partial(pack_kernel, experts),
        out_shape=jax.ShapeDtypeStruct((experts * 3 // 4, tokens.shape[1] + LANES), jnp.bfloat16),
        in_specs=[pl.BlockSpec(memory_space=pltpu.HBM)] * 3,
        out_specs=in_vmem,
        scratch_shapes=[
            pltpu.VMEM(tokens.shape, tokens.dtype),
            pltpu.VMEM(expert_ids.shape[::-1], expert_ids.dtype),
            pltpu.VMEM(gate_values.shape[::-1], gate_values.dtype),
            pltpu.SemaphoreType.DMA((PACK_PARTS + 2,)),
        ],
        compiler_params=pltpu.CompilerParams(vmem_limit_bytes=PACK_LIMIT * MIB),
        name="pack",
    )(tokens, expert_ids.T, gate_values.T)


def expert_kernel(held, *refs):
    pieces, weights, refs = refs[:4], refs[4:7], refs[7:]
    terms_ref, hidden_ref, refs = refs[0], refs[1], refs[2:]
    rows = refs[0] if held else refs[3]
    count, width = rows.shape
    part = count // 4
    loads = [(), (), ()]
    if not held:
        units, sems = weights[0].shape[0], refs[4]
        loads = [
            [
                pltpu.make_async_copy(
                    src.at[pl.ds(s * units // PARTS, units // PARTS)],
                    dst.at[pl.ds(s * units // PARTS, units // PARTS)],
                    sems.at[PARTS * k + s],
                )
                for s in range(PARTS)
            ]
            for k, (src, dst) in enumerate(zip(weights, refs[:3]))
        ]
        weights = refs[:3]
    for weight in loads:
        for load in weight:
            load.start()
    for p in range(4):
        rows[p * part : (p + 1) * part] = pieces[p][:, :width]
    gates = jnp.concatenate([piece[:, width:] for piece in pieces], axis=0).astype(jnp.float32)
    lane = lax.broadcasted_iota(jnp.int32, gates.shape, 1)
    gates = jnp.where(lane == lax.axis_index("expert"), gates, 0.0)
    gate = jnp.sum(gates, axis=1, keepdims=True)
    contract = (((1,), (1,)), ((), ()))
    products = []
    for k in range(2):
        for load in loads[k]:
            load.wait()
        products.append(
            lax.dot_general(
                rows[...], weights[k][...], contract, preferred_element_type=jnp.float32
            )
        )
    hidden = (gate * (jax.nn.silu(products[0]) * products[1])).astype(jnp.bfloat16)
    hidden_ref[...] = hidden
    for load in loads[2]:
        load.wait()
    for start in range(0, width, BLOCK):
        span = slice(start, start + BLOCK)
        terms = jnp.dot(hidden, weights[2][:, span], preferred_element_type=jnp.float32)
        terms_ref[:, span] = terms.astype(jnp.bfloat16)


def expert_terms(pieces, weights, held):
    units, width = weights[0].shape
    count = 4 * pieces[0].shape[0]
    in_vmem = pl.BlockSpec(memory_space=pltpu.VMEM)
    in_hbm = pl.BlockSpec(memory_space=pltpu.HBM)
    out_shape = [
        jax.ShapeDtypeStruct((count, width), jnp.bfloat16),
        jax.ShapeDtypeStruct((count, units), jnp.bfloat16),
    ]
    scratch = [pltpu.VMEM((count, width), jnp.bfloat16)]
    if not held:
        out_shape += [jax.ShapeDtypeStruct((units, width), jnp.bfloat16)] * 3
        scratch += [pltpu.SemaphoreType.DMA((3 * PARTS,))]
    return pl.pallas_call(
        functools.partial(expert_kernel, held),
        out_shape=out_shape,
        in_specs=[in_vmem] * 4 + [in_vmem if held else in_hbm] * 3,
        out_specs=[in_vmem] * len(out_shape),
        scratch_shapes=scratch,
        compiler_params=pltpu.CompilerParams(vmem_limit_bytes=(16 if held else LIMIT) * MIB),
        cost_estimate=pl.CostEstimate(
            flops=6 * count * units * width,
            bytes_accessed=8 * units * width,
            transcendentals=count * units,
        ),
        name="expert_terms",
    )(*pieces, *weights)


def turn_kernel(first_ref, second_ref, out_ref):
    hidden = jnp.concatenate([first_ref[...], second_ref[...]], axis=0)
    out_ref[...] = hidden.astype(jnp.float32).T.astype(jnp.bfloat16)


def turn(first, second):
    return pl.pallas_call(
        turn_kernel,
        out_shape=jax.ShapeDtypeStruct((first.shape[1], 2 * first.shape[0]), jnp.bfloat16),
        in_specs=[pl.BlockSpec(memory_space=pltpu.VMEM)] * 2,
        out_specs=pl.BlockSpec(memory_space=pltpu.VMEM),
        compiler_params=pltpu.CompilerParams(vmem_limit_bytes=8 * MIB),
        cost_estimate=pl.CostEstimate(
            flops=0, bytes_accessed=8 * first.size, transcendentals=0
        ),
        name="turn",
    )(first, second)


def update_kernel(*refs):
    pieces = refs[:8]
    hidden_t_ref, down_ref, first_ref, second_ref = refs[8:12]
    outs, held, sems = refs[12:15], refs[15:18], refs[18]
    root = (1.0 - second_decay**adam_count) ** 0.5
    rate = learn_rate * root / (1.0 - first_decay**adam_count)
    keep = 1.0 - learn_rate * weight_decay
    stores = []
    for start in range(0, down_ref.shape[1], UPDATE_BLOCK):
        span = pl.ds(start, UPDATE_BLOCK)
        cotangent = jnp.concatenate([piece[:, span] for piece in pieces], axis=0)
        gradient = jnp.dot(hidden_t_ref[...], cotangent, preferred_element_type=jnp.float32)
        first = first_decay * first_ref[:, span].astype(jnp.float32)
        first += (1.0 - first_decay) * gradient
        second = second_decay * second_ref[:, span].astype(jnp.float32)
        second += (1.0 - second_decay) * gradient * gradient
        step = rate * first / (jnp.sqrt(second) + adam_epsilon * root)
        down = keep * down_ref[:, span].astype(jnp.float32) - step
        for k, value in enumerate((down, first, second)):
            held[k][:, span] = value.astype(jnp.bfloat16)
            stores.append(
                pltpu.make_async_copy(
                    held[k].at[:, span], outs[k].at[:, span], sems.at[len(stores)]
                )
            )
            stores[-1].start()
    for store in stores:
        store.wait()


def update(pieces, hidden_t, down_weight, first_moment, second_moment):
    units, width = down_weight.shape
    part = pieces[0].shape[0]
    return pl.pallas_call(
        update_kernel,
        out_shape=[jax.ShapeDtypeStruct((units, width), jnp.bfloat16)] * 3,
        in_specs=[pl.BlockSpec(memory_space=pltpu.VMEM)] * 12,
        out_specs=[pl.BlockSpec(memory_space=pltpu.HBM)] * 3,
        scratch_shapes=[pltpu.VMEM((units, width), jnp.bfloat16)] * 3
        + [pltpu.SemaphoreType.DMA((3 * width // UPDATE_BLOCK,))],
        compiler_params=pltpu.CompilerParams(vmem_limit_bytes=24 * MIB),
        cost_estimate=pl.CostEstimate(
            flops=2 * 8 * part * units * width,
            bytes_accessed=14 * units * width,
            transcendentals=2 * units * width,
        ),
        name="update",
    )(*pieces, hidden_t, down_weight, first_moment, second_moment)


def dense_plan(
    tokens,
    expert_ids,
    gate_values,
    gate_weight,
    up_weight,
    down_weight,
    first_moment,
    second_moment,
):
    experts = lax.axis_size("expert")
    width = tokens.shape[1]
    pieces = spread(pack(tokens, expert_ids, gate_values, experts))
    pair_tokens = pieces[0][: 2 * (experts * 3 // 4), :width].astype(jnp.float32)
    pieces += to_core(pieces)
    weights = (gate_weight[0], up_weight[0], down_weight[0])
    own, own_hidden, *held = expert_terms(pieces[:4], weights, False)
    other, other_hidden = expert_terms(pieces[4:], held, True)
    hidden_t = turn(own_hidden, other_hidden)
    cotangent = jnp.tanh(pair_tokens + collect(own, other)).astype(jnp.bfloat16)
    cotangent = jnp.concatenate([cotangent, swap(cotangent, LINE[1])], axis=0)
    pieces = across(cotangent)
    pieces += to_core(pieces)
    outs = update(pieces, hidden_t, down_weight[0], first_moment[0], second_moment[0])
    return tuple(out[None] for out in outs)


def solution(mesh):
    in_specs = (
        P(("dp", "expert"), None),
        P(("dp", "expert"), None),
        P(("dp", "expert"), None),
        P("expert", "dp", None),
        P("expert", "dp", None),
        P("expert", "dp", None),
        P("expert", "dp", None),
        P("expert", "dp", None),
    )
    out_specs = (P("expert", "dp", None), P("expert", "dp", None), P("expert", "dp", None))
    small = mesh.shape["dp"] == 2 and mesh.shape["expert"] == 16
    local = dense_plan if small else slot_plan
    return jax.shard_map(local, mesh=mesh, in_specs=in_specs, out_specs=out_specs, check_vma=False)
```

```python
import functools

import jax
import jax.numpy as jnp
from jax import lax
from jax.experimental import pallas as pl
from jax.experimental.pallas import tpu as pltpu
from jax.sharding import PartitionSpec as P

CAP = 6


first_decay = 0.9
second_decay = 0.95
learn_rate = 0.00024
weight_decay = 0.1
adam_epsilon = 1e-08
adam_count = 100.0


def slot_table(id_block, gate_block, experts, capacity):
    numbers = jnp.arange(experts, dtype=jnp.int32)
    matches = id_block[:, :, None] == numbers[None, None, :]
    member = jnp.sum(matches.astype(jnp.int32), axis=1)
    chosen = jnp.sum(
        jnp.where(matches, gate_block[:, :, None].astype(jnp.float32), jnp.float32(0.0)), axis=1
    )
    position = jnp.cumsum(member, axis=0) - member
    slot_ids = jnp.arange(capacity, dtype=jnp.int32)
    onehot = member[:, :, None] * (position[:, :, None] == slot_ids[None, None, :]).astype(
        jnp.int32
    )
    return (onehot, chosen)


def expert_hidden(expert_rows, gate_rows, up_rows):
    contract = (((1,), (1,)), ((), ()))
    gate_part = lax.dot_general(
        expert_rows, gate_rows, contract, preferred_element_type=jnp.float32
    )
    up_part = lax.dot_general(expert_rows, up_rows, contract, preferred_element_type=jnp.float32)
    return (jax.nn.silu(gate_part) * up_part).astype(jnp.bfloat16)


def adam_update(gradient, weight_rows, first_rows, second_rows):
    first_new = first_decay * first_rows.astype(jnp.float32) + (1.0 - first_decay) * gradient
    second_new = (
        second_decay * second_rows.astype(jnp.float32) + (1.0 - second_decay) * gradient * gradient
    )
    first_hat = first_new / (1.0 - first_decay**adam_count)
    second_hat = second_new / (1.0 - second_decay**adam_count)
    weight_new = weight_rows.astype(jnp.float32) * (
        1.0 - learn_rate * weight_decay
    ) - learn_rate * first_hat / (jnp.sqrt(second_hat) + adam_epsilon)
    return (
        weight_new.astype(jnp.bfloat16),
        first_new.astype(jnp.bfloat16),
        second_new.astype(jnp.bfloat16),
    )


def slot_plan(
    tokens,
    expert_ids,
    gate_values,
    gate_weight,
    up_weight,
    down_weight,
    first_moment,
    second_moment,
):
    experts = lax.axis_size("expert")
    tok_count, model_width = tokens.shape
    capacity = CAP
    slot_count = experts * capacity
    onehot, chosen = slot_table(expert_ids, gate_values, experts, capacity)
    dispatch_map = onehot.reshape(tok_count, slot_count).astype(jnp.bfloat16)
    combine_map = (
        (onehot.astype(jnp.float32) * chosen[:, :, None])
        .reshape(tok_count, slot_count)
        .astype(jnp.bfloat16)
    )
    over_tokens = (((0,), (0,)), ((), ()))
    outgoing = lax.dot_general(
        dispatch_map, tokens, over_tokens, preferred_element_type=jnp.float32
    ).astype(jnp.bfloat16)
    arrived = lax.all_to_all(
        outgoing.reshape(experts, capacity, model_width),
        "expert",
        split_axis=0,
        concat_axis=0,
        tiled=True,
    )
    arrived = arrived.reshape(slot_count, model_width)
    gate_full, up_full, down_full = (
        lax.all_gather(gate_weight, "dp", axis=1, tiled=True),
        lax.all_gather(up_weight, "dp", axis=1, tiled=True),
        lax.all_gather(down_weight, "dp", axis=1, tiled=True),
    )
    hidden = expert_hidden(arrived, gate_full[0], up_full[0])
    outputs = jnp.dot(hidden, down_full[0], preferred_element_type=jnp.float32).astype(jnp.bfloat16)
    returned = lax.all_to_all(
        outputs.reshape(experts, capacity, model_width),
        "expert",
        split_axis=0,
        concat_axis=0,
        tiled=True,
    )
    returned = returned.reshape(slot_count, model_width)
    mixed = jnp.dot(combine_map, returned, preferred_element_type=jnp.float32)
    cotangent = jnp.tanh(tokens.astype(jnp.float32) + mixed).astype(jnp.bfloat16)
    weighted = lax.dot_general(
        combine_map, cotangent, over_tokens, preferred_element_type=jnp.float32
    ).astype(jnp.bfloat16)
    arrived_grad = lax.all_to_all(
        weighted.reshape(experts, capacity, model_width),
        "expert",
        split_axis=0,
        concat_axis=0,
        tiled=True,
    )
    arrived_grad = arrived_grad.reshape(slot_count, model_width)
    gradient = lax.psum_scatter(
        lax.dot_general(
            hidden, arrived_grad, over_tokens, preferred_element_type=jnp.float32
        ).astype(jnp.bfloat16),
        "dp",
        scatter_dimension=0,
        tiled=True,
    ).astype(jnp.float32)
    new_down, new_first, new_second = adam_update(
        gradient, down_weight[0], first_moment[0], second_moment[0]
    )
    return (new_down[None], new_first[None], new_second[None])


AXES = ("dp", "expert")
CORE = 1
PLANE = (2, 16, 18)
LINE = (8, 4, 12)
BLOCK = 512
UPDATE_BLOCK = 256
PARTS = 4
LIMIT = 46
PACK_PARTS = 4
PACK_LIMIT = 60
LANES = 128
MIB = 1024 * 1024


def swap(block, mask):
    count = lax.axis_size(AXES)
    return lax.ppermute(block, AXES, [(i, i ^ mask) for i in range(count)])


def spread(block):
    block = jnp.concatenate([block] + [swap(block, mask) for mask in LINE], axis=0)
    return across(block)


def across(block):
    return [block] + [swap(block, mask) for mask in PLANE]


def to_core(pieces):
    return [swap(piece, CORE) for piece in pieces]


def add_parts(own, other_parts):
    total = own.astype(jnp.float32)
    for part in other_parts:
        total = total + part.astype(jnp.float32)
    return total


def collect(own, other):
    rows = own.shape[0] // (len(PLANE) + 1)
    half = own.shape[1] // 2
    both = add_parts(own[3 * rows :], [swap(other[1], CORE)])
    own, first, second = jnp.split(add_parts(own[: 3 * rows], [swap(other[0], CORE)]), 3, axis=0)
    low = swap(both[:, :half].astype(jnp.bfloat16), PLANE[0])
    high = swap(both[:, half:].astype(jnp.bfloat16), PLANE[1])
    first = jnp.concatenate([first[:, :half], add_parts(first[:, half:], [high])], axis=1)
    second = jnp.concatenate([add_parts(second[:, :half], [low]), second[:, half:]], axis=1)
    sent = [swap(first.astype(jnp.bfloat16), PLANE[0]), swap(second.astype(jnp.bfloat16), PLANE[1])]
    kept, sent = jnp.split(add_parts(own, sent), 2, axis=0)
    pair = add_parts(kept, [swap(sent.astype(jnp.bfloat16), LINE[1])]).astype(jnp.bfloat16)
    mine, its = jnp.split(pair, 2, axis=0)
    return add_parts(pair, [swap(jnp.concatenate([its, mine], axis=0), LINE[0])])


def pack_kernel(experts, tokens_ref, ids_ref, gates_ref, out_ref, *scratch):
    tokens_vm, ids_vm, gates_vm, sems = scratch
    count, width = tokens_vm.shape
    part = count // PACK_PARTS
    loads = [
        pltpu.make_async_copy(
            tokens_ref.at[pl.ds(k * part, part)], tokens_vm.at[pl.ds(k * part, part)], sems.at[k]
        )
        for k in range(PACK_PARTS)
    ]
    ids_load = pltpu.make_async_copy(ids_ref, ids_vm, sems.at[PACK_PARTS])
    gates_load = pltpu.make_async_copy(gates_ref, gates_vm, sems.at[PACK_PARTS + 1])
    for load in [ids_load, gates_load] + loads:
        load.start()
    ids_load.wait()
    gates_load.wait()
    ids, values = ids_vm[...], gates_vm[...].astype(jnp.float32)
    row = lax.broadcasted_iota(jnp.int32, (LANES, count), 0)
    gates = jnp.zeros((LANES, count), jnp.float32)
    hot = jnp.zeros((LANES, count), jnp.bool_)
    for k in range(ids.shape[0]):
        named = jnp.broadcast_to(ids[k : k + 1], row.shape)
        gates += jnp.where((named == row) & (row < experts), values[k : k + 1], 0.0)
        hot |= named < experts
    source = lax.broadcasted_iota(jnp.int32, (count, count), 0)
    target = lax.broadcasted_iota(jnp.int32, (count, count), 1)
    before = jnp.where(source < target, 1.0, 0.0).astype(jnp.bfloat16)
    marks = jnp.where(hot, 1.0, 0.0).astype(jnp.bfloat16)
    rank = jnp.dot(marks, before, preferred_element_type=jnp.float32)
    pick = jnp.where(hot & (rank.astype(jnp.int32) == row), 1.0, 0.0).astype(jnp.bfloat16)
    rows = out_ref.shape[0]
    pick = pick[: 16 * pl.cdiv(rows, 16)]
    hot_gates = lax.dot_general(
        pick,
        gates.astype(jnp.bfloat16),
        (((1,), (1,)), ((), ())),
        preferred_element_type=jnp.float32,
    )
    out_ref[:, width:] = hot_gates[:rows].astype(jnp.bfloat16)
    for load in loads:
        load.wait()
    hot_tokens = jnp.dot(pick, tokens_vm[...], preferred_element_type=jnp.float32)
    out_ref[:, :width] = hot_tokens[:rows].astype(jnp.bfloat16)


def pack(tokens, expert_ids, gate_values, experts):
    in_vmem = pl.BlockSpec(memory_space=pltpu.VMEM)
    return pl.pallas_call(
        functools.partial(pack_kernel, experts),
        out_shape=jax.ShapeDtypeStruct((experts * 3 // 4, tokens.shape[1] + LANES), jnp.bfloat16),
        in_specs=[pl.BlockSpec(memory_space=pltpu.HBM)] * 3,
        out_specs=in_vmem,
        scratch_shapes=[
            pltpu.VMEM(tokens.shape, tokens.dtype),
            pltpu.VMEM(expert_ids.shape[::-1], expert_ids.dtype),
            pltpu.VMEM(gate_values.shape[::-1], gate_values.dtype),
            pltpu.SemaphoreType.DMA((PACK_PARTS + 2,)),
        ],
        compiler_params=pltpu.CompilerParams(vmem_limit_bytes=PACK_LIMIT * MIB),
        name="pack",
    )(tokens, expert_ids.T, gate_values.T)


def expert_kernel(held, *refs):
    pieces, weights, refs = refs[:4], refs[4:7], refs[7:]
    groups = 2 if held else 1
    terms_refs, hidden_ref, refs = refs[:groups], refs[groups], refs[groups + 1 :]
    rows = refs[0] if held else refs[3]
    count, width = rows.shape
    part = count // 4
    loads = [(), (), ()]
    if not held:
        units, sems = weights[0].shape[0], refs[4]
        loads = [
            [
                pltpu.make_async_copy(
                    src.at[pl.ds(s * units // PARTS, units // PARTS)],
                    dst.at[pl.ds(s * units // PARTS, units // PARTS)],
                    sems.at[PARTS * k + s],
                )
                for s in range(PARTS)
            ]
            for k, (src, dst) in enumerate(zip(weights, refs[:3]))
        ]
        weights = refs[:3]
    for weight in loads:
        for load in weight:
            load.start()
    for p in range(4):
        rows[p * part : (p + 1) * part] = pieces[p][:, :width]
    gates = jnp.concatenate([piece[:, width:] for piece in pieces], axis=0).astype(jnp.float32)
    lane = lax.broadcasted_iota(jnp.int32, gates.shape, 1)
    gates = jnp.where(lane == lax.axis_index("expert"), gates, 0.0)
    gate = jnp.sum(gates, axis=1, keepdims=True)
    contract = (((1,), (1,)), ((), ()))
    products = []
    for k in range(2):
        for load in loads[k]:
            load.wait()
        products.append(
            lax.dot_general(
                rows[...], weights[k][...], contract, preferred_element_type=jnp.float32
            )
        )
    hidden = (gate * (jax.nn.silu(products[0]) * products[1])).astype(jnp.bfloat16)
    hidden_ref[...] = hidden
    for load in loads[2]:
        load.wait()
    for start in range(0, width, BLOCK):
        span = slice(start, start + BLOCK)
        terms = jnp.dot(hidden, weights[2][:, span], preferred_element_type=jnp.float32)
        terms, done = terms.astype(jnp.bfloat16), 0
        for terms_ref in terms_refs:
            size = terms_ref.shape[0]
            terms_ref[:, span] = terms[done : done + size]
            done += size


def expert_terms(pieces, weights, held):
    units, width = weights[0].shape
    count = 4 * pieces[0].shape[0]
    in_vmem = pl.BlockSpec(memory_space=pltpu.VMEM)
    in_hbm = pl.BlockSpec(memory_space=pltpu.HBM)
    groups = [count * 3 // 4, count // 4] if held else [count]
    out_shape = [jax.ShapeDtypeStruct((size, width), jnp.bfloat16) for size in groups]
    out_shape += [jax.ShapeDtypeStruct((count, units), jnp.bfloat16)]
    scratch = [pltpu.VMEM((count, width), jnp.bfloat16)]
    if not held:
        out_shape += [jax.ShapeDtypeStruct((units, width), jnp.bfloat16)] * 3
        scratch += [pltpu.SemaphoreType.DMA((3 * PARTS,))]
    return pl.pallas_call(
        functools.partial(expert_kernel, held),
        out_shape=out_shape,
        in_specs=[in_vmem] * 4 + [in_vmem if held else in_hbm] * 3,
        out_specs=[in_vmem] * len(out_shape),
        scratch_shapes=scratch,
        compiler_params=pltpu.CompilerParams(vmem_limit_bytes=(16 if held else LIMIT) * MIB),
        cost_estimate=pl.CostEstimate(
            flops=6 * count * units * width,
            bytes_accessed=8 * units * width,
            transcendentals=count * units,
        ),
        name="expert_terms",
    )(*pieces, *weights)


def turn_kernel(first_ref, second_ref, out_ref):
    hidden = jnp.concatenate([first_ref[...], second_ref[...]], axis=0)
    out_ref[...] = hidden.astype(jnp.float32).T.astype(jnp.bfloat16)


def turn(first, second):
    return pl.pallas_call(
        turn_kernel,
        out_shape=jax.ShapeDtypeStruct((first.shape[1], 2 * first.shape[0]), jnp.bfloat16),
        in_specs=[pl.BlockSpec(memory_space=pltpu.VMEM)] * 2,
        out_specs=pl.BlockSpec(memory_space=pltpu.VMEM),
        compiler_params=pltpu.CompilerParams(vmem_limit_bytes=8 * MIB),
        cost_estimate=pl.CostEstimate(
            flops=0, bytes_accessed=8 * first.size, transcendentals=0
        ),
        name="turn",
    )(first, second)


def update_kernel(*refs):
    pieces = refs[:8]
    hidden_t_ref, down_ref, first_ref, second_ref = refs[8:12]
    outs, held, sems = refs[12:15], refs[15:18], refs[18]
    root = (1.0 - second_decay**adam_count) ** 0.5
    rate = learn_rate * root / (1.0 - first_decay**adam_count)
    keep = 1.0 - learn_rate * weight_decay
    stores = []
    for start in range(0, down_ref.shape[1], UPDATE_BLOCK):
        span = pl.ds(start, UPDATE_BLOCK)
        cotangent = jnp.concatenate([piece[:, span] for piece in pieces], axis=0)
        gradient = jnp.dot(hidden_t_ref[...], cotangent, preferred_element_type=jnp.float32)
        first = first_decay * first_ref[:, span].astype(jnp.float32)
        first += (1.0 - first_decay) * gradient
        second = second_decay * second_ref[:, span].astype(jnp.float32)
        second += (1.0 - second_decay) * gradient * gradient
        step = rate * first / (jnp.sqrt(second) + adam_epsilon * root)
        down = keep * down_ref[:, span].astype(jnp.float32) - step
        for k, value in enumerate((down, first, second)):
            held[k][:, span] = value.astype(jnp.bfloat16)
            stores.append(
                pltpu.make_async_copy(
                    held[k].at[:, span], outs[k].at[:, span], sems.at[len(stores)]
                )
            )
            stores[-1].start()
    for store in stores:
        store.wait()


def update(pieces, hidden_t, down_weight, first_moment, second_moment):
    units, width = down_weight.shape
    part = pieces[0].shape[0]
    return pl.pallas_call(
        update_kernel,
        out_shape=[jax.ShapeDtypeStruct((units, width), jnp.bfloat16)] * 3,
        in_specs=[pl.BlockSpec(memory_space=pltpu.VMEM)] * 12,
        out_specs=[pl.BlockSpec(memory_space=pltpu.HBM)] * 3,
        scratch_shapes=[pltpu.VMEM((units, width), jnp.bfloat16)] * 3
        + [pltpu.SemaphoreType.DMA((3 * width // UPDATE_BLOCK,))],
        compiler_params=pltpu.CompilerParams(vmem_limit_bytes=24 * MIB),
        cost_estimate=pl.CostEstimate(
            flops=2 * 8 * part * units * width,
            bytes_accessed=14 * units * width,
            transcendentals=2 * units * width,
        ),
        name="update",
    )(*pieces, hidden_t, down_weight, first_moment, second_moment)


def dense_plan(
    tokens,
    expert_ids,
    gate_values,
    gate_weight,
    up_weight,
    down_weight,
    first_moment,
    second_moment,
):
    experts = lax.axis_size("expert")
    width = tokens.shape[1]
    pieces = spread(pack(tokens, expert_ids, gate_values, experts))
    pair_tokens = pieces[0][: 2 * (experts * 3 // 4), :width].astype(jnp.float32)
    pieces += to_core(pieces)
    weights = (gate_weight[0], up_weight[0], down_weight[0])
    own, own_hidden, *held = expert_terms(pieces[:4], weights, False)
    *other, other_hidden = expert_terms(pieces[4:], held, True)
    hidden_t = turn(own_hidden, other_hidden)
    cotangent = jnp.tanh(pair_tokens + collect(own, other)).astype(jnp.bfloat16)
    cotangent = jnp.concatenate([cotangent, swap(cotangent, LINE[1])], axis=0)
    pieces = across(cotangent)
    pieces += to_core(pieces)
    outs = update(pieces, hidden_t, down_weight[0], first_moment[0], second_moment[0])
    return tuple(out[None] for out in outs)


def solution(mesh):
    in_specs = (
        P(("dp", "expert"), None),
        P(("dp", "expert"), None),
        P(("dp", "expert"), None),
        P("expert", "dp", None),
        P("expert", "dp", None),
        P("expert", "dp", None),
        P("expert", "dp", None),
        P("expert", "dp", None),
    )
    out_specs = (P("expert", "dp", None), P("expert", "dp", None), P("expert", "dp", None))
    small = mesh.shape["dp"] == 2 and mesh.shape["expert"] == 16
    local = dense_plan if small else slot_plan
    return jax.shard_map(local, mesh=mesh, in_specs=in_specs, out_specs=out_specs, check_vma=False)
```

```python
import functools

import jax
import jax.numpy as jnp
from jax import lax
from jax.experimental import pallas as pl
from jax.experimental.pallas import tpu as pltpu
from jax.sharding import PartitionSpec as P

CAP = 6


first_decay = 0.9
second_decay = 0.95
learn_rate = 0.00024
weight_decay = 0.1
adam_epsilon = 1e-08
adam_count = 100.0


def slot_table(id_block, gate_block, experts, capacity):
    numbers = jnp.arange(experts, dtype=jnp.int32)
    matches = id_block[:, :, None] == numbers[None, None, :]
    member = jnp.sum(matches.astype(jnp.int32), axis=1)
    chosen = jnp.sum(
        jnp.where(matches, gate_block[:, :, None].astype(jnp.float32), jnp.float32(0.0)), axis=1
    )
    position = jnp.cumsum(member, axis=0) - member
    slot_ids = jnp.arange(capacity, dtype=jnp.int32)
    onehot = member[:, :, None] * (position[:, :, None] == slot_ids[None, None, :]).astype(
        jnp.int32
    )
    return (onehot, chosen)


def expert_hidden(expert_rows, gate_rows, up_rows):
    contract = (((1,), (1,)), ((), ()))
    gate_part = lax.dot_general(
        expert_rows, gate_rows, contract, preferred_element_type=jnp.float32
    )
    up_part = lax.dot_general(expert_rows, up_rows, contract, preferred_element_type=jnp.float32)
    return (jax.nn.silu(gate_part) * up_part).astype(jnp.bfloat16)


def adam_update(gradient, weight_rows, first_rows, second_rows):
    first_new = first_decay * first_rows.astype(jnp.float32) + (1.0 - first_decay) * gradient
    second_new = (
        second_decay * second_rows.astype(jnp.float32) + (1.0 - second_decay) * gradient * gradient
    )
    first_hat = first_new / (1.0 - first_decay**adam_count)
    second_hat = second_new / (1.0 - second_decay**adam_count)
    weight_new = weight_rows.astype(jnp.float32) * (
        1.0 - learn_rate * weight_decay
    ) - learn_rate * first_hat / (jnp.sqrt(second_hat) + adam_epsilon)
    return (
        weight_new.astype(jnp.bfloat16),
        first_new.astype(jnp.bfloat16),
        second_new.astype(jnp.bfloat16),
    )


def slot_plan(
    tokens,
    expert_ids,
    gate_values,
    gate_weight,
    up_weight,
    down_weight,
    first_moment,
    second_moment,
):
    experts = lax.axis_size("expert")
    tok_count, model_width = tokens.shape
    capacity = CAP
    slot_count = experts * capacity
    onehot, chosen = slot_table(expert_ids, gate_values, experts, capacity)
    dispatch_map = onehot.reshape(tok_count, slot_count).astype(jnp.bfloat16)
    combine_map = (
        (onehot.astype(jnp.float32) * chosen[:, :, None])
        .reshape(tok_count, slot_count)
        .astype(jnp.bfloat16)
    )
    over_tokens = (((0,), (0,)), ((), ()))
    outgoing = lax.dot_general(
        dispatch_map, tokens, over_tokens, preferred_element_type=jnp.float32
    ).astype(jnp.bfloat16)
    arrived = lax.all_to_all(
        outgoing.reshape(experts, capacity, model_width),
        "expert",
        split_axis=0,
        concat_axis=0,
        tiled=True,
    )
    arrived = arrived.reshape(slot_count, model_width)
    gate_full, up_full, down_full = (
        lax.all_gather(gate_weight, "dp", axis=1, tiled=True),
        lax.all_gather(up_weight, "dp", axis=1, tiled=True),
        lax.all_gather(down_weight, "dp", axis=1, tiled=True),
    )
    hidden = expert_hidden(arrived, gate_full[0], up_full[0])
    outputs = jnp.dot(hidden, down_full[0], preferred_element_type=jnp.float32).astype(jnp.bfloat16)
    returned = lax.all_to_all(
        outputs.reshape(experts, capacity, model_width),
        "expert",
        split_axis=0,
        concat_axis=0,
        tiled=True,
    )
    returned = returned.reshape(slot_count, model_width)
    mixed = jnp.dot(combine_map, returned, preferred_element_type=jnp.float32)
    cotangent = jnp.tanh(tokens.astype(jnp.float32) + mixed).astype(jnp.bfloat16)
    weighted = lax.dot_general(
        combine_map, cotangent, over_tokens, preferred_element_type=jnp.float32
    ).astype(jnp.bfloat16)
    arrived_grad = lax.all_to_all(
        weighted.reshape(experts, capacity, model_width),
        "expert",
        split_axis=0,
        concat_axis=0,
        tiled=True,
    )
    arrived_grad = arrived_grad.reshape(slot_count, model_width)
    gradient = lax.psum_scatter(
        lax.dot_general(
            hidden, arrived_grad, over_tokens, preferred_element_type=jnp.float32
        ).astype(jnp.bfloat16),
        "dp",
        scatter_dimension=0,
        tiled=True,
    ).astype(jnp.float32)
    new_down, new_first, new_second = adam_update(
        gradient, down_weight[0], first_moment[0], second_moment[0]
    )
    return (new_down[None], new_first[None], new_second[None])


AXES = ("dp", "expert")
CORE = 1
PLANE = (2, 16, 18)
LINE = (8, 4, 12)
BLOCK = 512
UPDATE_BLOCK = 512
PARTS = 4
LIMIT = 46
PACK_PARTS = 4
PACK_LIMIT = 60
LANES = 128
MIB = 1024 * 1024


def swap(block, mask):
    count = lax.axis_size(AXES)
    return lax.ppermute(block, AXES, [(i, i ^ mask) for i in range(count)])


def spread(block):
    block = jnp.concatenate([block] + [swap(block, mask) for mask in LINE], axis=0)
    return across(block)


def across(block):
    return [block] + [swap(block, mask) for mask in PLANE]


def to_core(pieces):
    return [swap(piece, CORE) for piece in pieces]


def add_parts(own, other_parts):
    total = own.astype(jnp.float32)
    for part in other_parts:
        total = total + part.astype(jnp.float32)
    return total


def collect(own, other):
    rows = own.shape[0] // (len(PLANE) + 1)
    half = own.shape[1] // 2
    both = add_parts(own[3 * rows :], [swap(other[1], CORE)])
    own, first, second = jnp.split(add_parts(own[: 3 * rows], [swap(other[0], CORE)]), 3, axis=0)
    low = swap(both[:, :half].astype(jnp.bfloat16), PLANE[0])
    high = swap(both[:, half:].astype(jnp.bfloat16), PLANE[1])
    first = jnp.concatenate([first[:, :half], add_parts(first[:, half:], [high])], axis=1)
    second = jnp.concatenate([add_parts(second[:, :half], [low]), second[:, half:]], axis=1)
    sent = [swap(first.astype(jnp.bfloat16), PLANE[0]), swap(second.astype(jnp.bfloat16), PLANE[1])]
    kept, sent = jnp.split(add_parts(own, sent), 2, axis=0)
    pair = add_parts(kept, [swap(sent.astype(jnp.bfloat16), LINE[1])]).astype(jnp.bfloat16)
    mine, its = jnp.split(pair, 2, axis=0)
    return add_parts(pair, [swap(jnp.concatenate([its, mine], axis=0), LINE[0])])


def pack_kernel(experts, tokens_ref, ids_ref, gates_ref, out_ref, *scratch):
    tokens_vm, ids_vm, gates_vm, sems = scratch
    count, width = tokens_vm.shape
    part = count // PACK_PARTS
    loads = [
        pltpu.make_async_copy(
            tokens_ref.at[pl.ds(k * part, part)], tokens_vm.at[pl.ds(k * part, part)], sems.at[k]
        )
        for k in range(PACK_PARTS)
    ]
    ids_load = pltpu.make_async_copy(ids_ref, ids_vm, sems.at[PACK_PARTS])
    gates_load = pltpu.make_async_copy(gates_ref, gates_vm, sems.at[PACK_PARTS + 1])
    for load in [ids_load, gates_load] + loads:
        load.start()
    ids_load.wait()
    gates_load.wait()
    ids, values = ids_vm[...], gates_vm[...].astype(jnp.float32)
    row = lax.broadcasted_iota(jnp.int32, (LANES, count), 0)
    gates = jnp.zeros((LANES, count), jnp.float32)
    hot = jnp.zeros((LANES, count), jnp.bool_)
    for k in range(ids.shape[0]):
        named = jnp.broadcast_to(ids[k : k + 1], row.shape)
        gates += jnp.where((named == row) & (row < experts), values[k : k + 1], 0.0)
        hot |= named < experts
    source = lax.broadcasted_iota(jnp.int32, (count, count), 0)
    target = lax.broadcasted_iota(jnp.int32, (count, count), 1)
    before = jnp.where(source < target, 1.0, 0.0).astype(jnp.bfloat16)
    marks = jnp.where(hot, 1.0, 0.0).astype(jnp.bfloat16)
    rank = jnp.dot(marks, before, preferred_element_type=jnp.float32)
    pick = jnp.where(hot & (rank.astype(jnp.int32) == row), 1.0, 0.0).astype(jnp.bfloat16)
    rows = out_ref.shape[0]
    pick = pick[: 16 * pl.cdiv(rows, 16)]
    hot_gates = lax.dot_general(
        pick,
        gates.astype(jnp.bfloat16),
        (((1,), (1,)), ((), ())),
        preferred_element_type=jnp.float32,
    )
    out_ref[:, width:] = hot_gates[:rows].astype(jnp.bfloat16)
    for load in loads:
        load.wait()
    hot_tokens = jnp.dot(pick, tokens_vm[...], preferred_element_type=jnp.float32)
    out_ref[:, :width] = hot_tokens[:rows].astype(jnp.bfloat16)


def pack(tokens, expert_ids, gate_values, experts):
    in_vmem = pl.BlockSpec(memory_space=pltpu.VMEM)
    return pl.pallas_call(
        functools.partial(pack_kernel, experts),
        out_shape=jax.ShapeDtypeStruct((experts * 3 // 4, tokens.shape[1] + LANES), jnp.bfloat16),
        in_specs=[pl.BlockSpec(memory_space=pltpu.HBM)] * 3,
        out_specs=in_vmem,
        scratch_shapes=[
            pltpu.VMEM(tokens.shape, tokens.dtype),
            pltpu.VMEM(expert_ids.shape[::-1], expert_ids.dtype),
            pltpu.VMEM(gate_values.shape[::-1], gate_values.dtype),
            pltpu.SemaphoreType.DMA((PACK_PARTS + 2,)),
        ],
        compiler_params=pltpu.CompilerParams(vmem_limit_bytes=PACK_LIMIT * MIB),
        name="pack",
    )(tokens, expert_ids.T, gate_values.T)


def expert_kernel(held, *refs):
    pieces, weights, refs = refs[:4], refs[4:7], refs[7:]
    groups = 2 if held else 1
    terms_refs, hidden_ref, refs = refs[:groups], refs[groups], refs[groups + 1 :]
    rows = refs[0] if held else refs[3]
    count, width = rows.shape
    part = count // 4
    loads = [(), (), ()]
    if not held:
        units, sems = weights[0].shape[0], refs[4]
        loads = [
            [
                pltpu.make_async_copy(
                    src.at[pl.ds(s * units // PARTS, units // PARTS)],
                    dst.at[pl.ds(s * units // PARTS, units // PARTS)],
                    sems.at[PARTS * k + s],
                )
                for s in range(PARTS)
            ]
            for k, (src, dst) in enumerate(zip(weights, refs[:3]))
        ]
        weights = refs[:3]
    for weight in loads:
        for load in weight:
            load.start()
    for p in range(4):
        rows[p * part : (p + 1) * part] = pieces[p][:, :width]
    gates = jnp.concatenate([piece[:, width:] for piece in pieces], axis=0).astype(jnp.float32)
    lane = lax.broadcasted_iota(jnp.int32, gates.shape, 1)
    gates = jnp.where(lane == lax.axis_index("expert"), gates, 0.0)
    gate = jnp.sum(gates, axis=1, keepdims=True)
    contract = (((1,), (1,)), ((), ()))
    products = []
    for k in range(2):
        for load in loads[k]:
            load.wait()
        products.append(
            lax.dot_general(
                rows[...], weights[k][...], contract, preferred_element_type=jnp.float32
            )
        )
    hidden = (gate * (jax.nn.silu(products[0]) * products[1])).astype(jnp.bfloat16)
    hidden_ref[...] = hidden
    for load in loads[2]:
        load.wait()
    for start in range(0, width, BLOCK):
        span = slice(start, start + BLOCK)
        terms = jnp.dot(hidden, weights[2][:, span], preferred_element_type=jnp.float32)
        terms, done = terms.astype(jnp.bfloat16), 0
        for terms_ref in terms_refs:
            size = terms_ref.shape[0]
            terms_ref[:, span] = terms[done : done + size]
            done += size


def expert_terms(pieces, weights, held):
    units, width = weights[0].shape
    count = 4 * pieces[0].shape[0]
    in_vmem = pl.BlockSpec(memory_space=pltpu.VMEM)
    in_hbm = pl.BlockSpec(memory_space=pltpu.HBM)
    groups = [count * 3 // 4, count // 4] if held else [count]
    out_shape = [jax.ShapeDtypeStruct((size, width), jnp.bfloat16) for size in groups]
    out_shape += [jax.ShapeDtypeStruct((count, units), jnp.bfloat16)]
    scratch = [pltpu.VMEM((count, width), jnp.bfloat16)]
    if not held:
        out_shape += [jax.ShapeDtypeStruct((units, width), jnp.bfloat16)] * 3
        scratch += [pltpu.SemaphoreType.DMA((3 * PARTS,))]
    return pl.pallas_call(
        functools.partial(expert_kernel, held),
        out_shape=out_shape,
        in_specs=[in_vmem] * 4 + [in_vmem if held else in_hbm] * 3,
        out_specs=[in_vmem] * len(out_shape),
        scratch_shapes=scratch,
        compiler_params=pltpu.CompilerParams(vmem_limit_bytes=(16 if held else LIMIT) * MIB),
        cost_estimate=pl.CostEstimate(
            flops=6 * count * units * width,
            bytes_accessed=8 * units * width,
            transcendentals=count * units,
        ),
        name="expert_terms",
    )(*pieces, *weights)


def turn_kernel(first_ref, second_ref, out_ref):
    hidden = jnp.concatenate([first_ref[...], second_ref[...]], axis=0)
    out_ref[...] = hidden.astype(jnp.float32).T.astype(jnp.bfloat16)


def turn(first, second):
    return pl.pallas_call(
        turn_kernel,
        out_shape=jax.ShapeDtypeStruct((first.shape[1], 2 * first.shape[0]), jnp.bfloat16),
        in_specs=[pl.BlockSpec(memory_space=pltpu.VMEM)] * 2,
        out_specs=pl.BlockSpec(memory_space=pltpu.VMEM),
        compiler_params=pltpu.CompilerParams(vmem_limit_bytes=8 * MIB),
        cost_estimate=pl.CostEstimate(
            flops=0, bytes_accessed=8 * first.size, transcendentals=0
        ),
        name="turn",
    )(first, second)


def update_kernel(*refs):
    pieces = refs[:8]
    hidden_t_ref, down_ref, first_ref, second_ref = refs[8:12]
    outs, held, sems = refs[12:15], refs[15:18], refs[18]
    root = (1.0 - second_decay**adam_count) ** 0.5
    rate = learn_rate * root / (1.0 - first_decay**adam_count)
    keep = 1.0 - learn_rate * weight_decay
    stores = []
    for start in range(0, down_ref.shape[1], UPDATE_BLOCK):
        span = pl.ds(start, UPDATE_BLOCK)
        cotangent = jnp.concatenate([piece[:, span] for piece in pieces], axis=0)
        gradient = jnp.dot(hidden_t_ref[...], cotangent, preferred_element_type=jnp.float32)
        first = first_decay * first_ref[:, span].astype(jnp.float32)
        first += (1.0 - first_decay) * gradient
        second = second_decay * second_ref[:, span].astype(jnp.float32)
        second += (1.0 - second_decay) * gradient * gradient
        step = rate * first / (second * lax.rsqrt(second) + adam_epsilon * root)
        down = keep * down_ref[:, span].astype(jnp.float32) - step
        for k, value in enumerate((down, first, second)):
            held[k][:, span] = value.astype(jnp.bfloat16)
            stores.append(
                pltpu.make_async_copy(
                    held[k].at[:, span], outs[k].at[:, span], sems.at[len(stores)]
                )
            )
            stores[-1].start()
    for store in stores:
        store.wait()


def update(pieces, hidden_t, down_weight, first_moment, second_moment):
    units, width = down_weight.shape
    part = pieces[0].shape[0]
    return pl.pallas_call(
        update_kernel,
        out_shape=[jax.ShapeDtypeStruct((units, width), jnp.bfloat16)] * 3,
        in_specs=[pl.BlockSpec(memory_space=pltpu.VMEM)] * 12,
        out_specs=[pl.BlockSpec(memory_space=pltpu.HBM)] * 3,
        scratch_shapes=[pltpu.VMEM((units, width), jnp.bfloat16)] * 3
        + [pltpu.SemaphoreType.DMA((3 * width // UPDATE_BLOCK,))],
        compiler_params=pltpu.CompilerParams(vmem_limit_bytes=24 * MIB),
        cost_estimate=pl.CostEstimate(
            flops=2 * 8 * part * units * width,
            bytes_accessed=14 * units * width,
            transcendentals=2 * units * width,
        ),
        name="update",
    )(*pieces, hidden_t, down_weight, first_moment, second_moment)


def dense_plan(
    tokens,
    expert_ids,
    gate_values,
    gate_weight,
    up_weight,
    down_weight,
    first_moment,
    second_moment,
):
    experts = lax.axis_size("expert")
    width = tokens.shape[1]
    pieces = spread(pack(tokens, expert_ids, gate_values, experts))
    pair_tokens = pieces[0][: 2 * (experts * 3 // 4), :width].astype(jnp.float32)
    pieces += to_core(pieces)
    weights = (gate_weight[0], up_weight[0], down_weight[0])
    own, own_hidden, *held = expert_terms(pieces[:4], weights, False)
    *other, other_hidden = expert_terms(pieces[4:], held, True)
    hidden_t = turn(own_hidden, other_hidden)
    cotangent = jnp.tanh(pair_tokens + collect(own, other)).astype(jnp.bfloat16)
    cotangent = jnp.concatenate([cotangent, swap(cotangent, LINE[1])], axis=0)
    pieces = across(cotangent)
    pieces += to_core(pieces)
    outs = update(pieces, hidden_t, down_weight[0], first_moment[0], second_moment[0])
    return tuple(out[None] for out in outs)


def solution(mesh):
    in_specs = (
        P(("dp", "expert"), None),
        P(("dp", "expert"), None),
        P(("dp", "expert"), None),
        P("expert", "dp", None),
        P("expert", "dp", None),
        P("expert", "dp", None),
        P("expert", "dp", None),
        P("expert", "dp", None),
    )
    out_specs = (P("expert", "dp", None), P("expert", "dp", None), P("expert", "dp", None))
    small = mesh.shape["dp"] == 2 and mesh.shape["expert"] == 16
    local = dense_plan if small else slot_plan
    return jax.shard_map(local, mesh=mesh, in_specs=in_specs, out_specs=out_specs, check_vma=False)
```
